32 devices in a mesh: lat: 8 (over z, y), tp: 4 (over x, core).
Axes of the slice: x: 2, y: 2, z: 4, core: 2. Of those that a mesh axis runs over, the one named last changes fastest.
Arguments:
- activations: bfloat16 [2048, 7168], P('lat', 'tp'), may hold values from -16 to 16, as said below
- active_blocks: int32 [2048, 2], P('lat'), may hold values from 0 to 7, all different within a row; in each aligned block of 256 rows (0 to 255, 256 to 511, ...) at most 128 rows name the same one
- enc_weight: bfloat16 [7168, 16384], P('tp', 'lat'), may hold values from -0.0625 to 0.0625
- enc_bias: float32 [16384], P('lat'), may hold values from -3 to 3
- dec_weight: bfloat16 [16384, 7168], P('lat', 'tp'), may hold values from -0.125 to 0.125
- dec_bias: float32 [7168], P('tp'), may hold values from -3 to 3
Outputs:
- token_error: float32 [2048], P('lat')
- mean_error: float32 [], replicated
The draws below stay inside these ranges and needn't reach their ends.
Inputs may be any that keep to these rules, and one draw needn't show every extreme that they name: `active_blocks`: each row names 2 different blocks; among the rows of one index of lat no block is named more than 128 times, and some block is named exactly 128 times. `activations`: real values.
All inputs are finite; a program needn't handle non-finite values.
Results may differ from the reference program's by a relative error of at most 0.005.
Values may be sent and summed in bfloat16 or wider, within the bound.
A program may use at most 64 MiB of HBM per device.

```python
import math
import jax
import jax.numpy as jnp
import numpy as np
from jax import lax

D = 7168
BLOCK = 2048
K_ACT = 2
TOK_DEV = 256
TOKENS = 2048
LATENTS = 16384
CAP = 128
N_LAT = 8
N_TP = 4


def draw_activations(key, part):
    position = jnp.arange(TOKENS, dtype=jnp.float32) / TOKENS
    row_scale = 0.25 * jnp.exp(position * jnp.log(10.0))
    values = jnp.clip(jax.random.normal(key, (TOKENS, D), jnp.float32), -6.0, 6.0)
    return (values * row_scale[:, None]).astype(jnp.bfloat16)


def levels(own_key, dims, shards, low, top_value):
    level = 1.0
    for dim, blocks in shards:
        steps = jax.random.uniform(jax.random.fold_in(jax.random.fold_in(own_key, 6), dim), (blocks,), jnp.float32, low / len(shards), top_value / len(shards))
        level = level * jnp.repeat(jnp.exp(steps), dims[dim] // blocks).reshape((-1,) + (1,) * (len(dims) - 1 - dim))
    return level


def deal_out(rng, own, number, rows, number_of, top, most, lean):
    sequence = jax.random.permutation(rng, number_of)
    crowded, common = portions_of(number_of, rows * top, most, lean, True), portions_of(number_of, rows * top, most, lean, False)
    places = jnp.arange(number_of)

    def named(sizes, offset_by):
        used = int((sizes > 0).sum())
        fixed = max(1, used // 4)
        shifted = fixed + (places - fixed + offset_by * (used - fixed)) % max(1, number_of - fixed)
        return jnp.zeros((number_of,), jnp.int32).at[sequence[jnp.where(places < fixed, places, shifted)]].set(jnp.asarray(sizes, jnp.int32))

    sizes = jnp.where(number % 4 == 0, named(crowded, number // 4), named(common, number - number // 4 - 1))
    mixed = jax.random.permutation(jax.random.fold_in(own, 3), number_of)
    donor, taker = mixed[0:number_of // 2 * 2:2], mixed[1:number_of // 2 * 2:2]
    slack = jnp.minimum(sizes[donor] - 1, most - sizes[taker]) // 2
    slack = jnp.where((donor == sequence[0]) | (taker == sequence[0]) | (sizes[taker] == 0), 0, jnp.maximum(slack, 0))
    shifted = jax.random.randint(jax.random.fold_in(own, 4), (number_of // 2,), 0, 1 << 20) % (slack + 1)
    sizes = sizes.at[donor].add(-shifted).at[taker].add(shifted)
    items = jnp.searchsorted(jnp.cumsum(sizes), jnp.arange(rows * top), side="right").astype(jnp.int32)
    table = items.reshape(top, rows).T
    table = table[jax.random.permutation(jax.random.fold_in(own, 1), rows)]
    offset_by = jax.random.randint(jax.random.fold_in(own, 2), (rows, 1), 0, top)
    return jnp.take_along_axis(table, (jnp.arange(top)[None, :] + offset_by) % top, axis=1)


def portions_of(count, total, most, skew, full):
    loads = [(1 << 20) // math.isqrt(rank ** skew) + 1 for rank in range(1, count + 1)]
    largest = most if full else min(most, max(-(-total // count), total * loads[0] // sum(loads)))
    least = 1 if total - largest >= count - 1 else 0
    holding, rest = [largest] + [least] * (count - 1), total - largest - least * (count - 1)
    while rest > 0:
        movable = [i for i in range(1, count) if holding[i] < largest] or [i for i in range(1, count) if holding[i] < most]
        pool, remaining = sum([loads[i] for i in movable]), rest
        for i in movable:
            extra = min(most - holding[i], max(1, remaining * loads[i] // pool), rest)
            holding[i] = holding[i] + extra
            rest = rest - extra
    return np.array(holding)


def gaussian(stream_key, dims, deviation, most, split=(), kind=jnp.bfloat16):
    array = deviation * jax.random.normal(stream_key, dims, jnp.float32)
    if split:
        array = array * levels(stream_key, dims, split, -0.22, 0.18)
    return jnp.clip(array, -most, most).astype(kind)


def setup_inputs(seed: int = 0) -> dict:
    seeds = jax.random.split(jax.random.key(seed), 7)
    activations = draw_activations(jax.random.fold_in(seeds[6], 71), 0)
    active_blocks_keys = jax.random.split(jax.random.fold_in(seeds[1], 1), TOKENS // TOK_DEV)
    active_blocks_turns = jax.random.permutation(jax.random.fold_in(seeds[1], 3), TOKENS // TOK_DEV)
    active_blocks = jax.vmap(lambda own, number: deal_out(jax.random.fold_in(seeds[1], 2), own, number, TOK_DEV, N_LAT, K_ACT, CAP, 2))(active_blocks_keys, active_blocks_turns).reshape((TOKENS, K_ACT))
    enc_weight = gaussian(seeds[2], (D, LATENTS), D ** -0.5, 0.0625, ((0, 4), (1, 8)))
    enc_bias = gaussian(seeds[3], (LATENTS,), 0.5, 3.0, ((0, 8),), jnp.float32)
    dec_weight = gaussian(seeds[4], (LATENTS, D), BLOCK ** -0.5, 0.125, ((0, 8), (1, 4)))
    dec_bias = gaussian(seeds[5], (D,), 0.5, 3.0, ((0, 4),), jnp.float32)
    return {"activations": activations, "active_blocks": active_blocks, "enc_weight": enc_weight, "enc_bias": enc_bias, "dec_weight": dec_weight, "dec_bias": dec_bias}


def reference(activations, active_blocks, enc_weight, enc_bias, dec_weight, dec_bias):
    width = activations.shape[1]
    part_width = width // N_TP
    centred = (activations.astype(jnp.float32) - dec_bias).astype(jnp.bfloat16)
    flat = active_blocks.reshape(-1).astype(jnp.int32)
    slots = CAP * N_LAT
    order = jnp.argsort(flat, stable=True).astype(jnp.int32)
    order = jnp.concatenate([order, jnp.zeros((slots,), jnp.int32)])
    counts = jnp.sum((flat[:, None] == jnp.arange(N_LAT, dtype=jnp.int32)[None, :]).astype(jnp.int32), axis=0)
    starts = (jnp.cumsum(counts) - counts).astype(jnp.int32)

    def one_block(index, total):
        picked = lax.dynamic_slice_in_dim(order, starts[index], slots)
        rows_of = (picked // K_ACT).astype(jnp.int32)
        valid = (jnp.arange(slots, dtype=jnp.int32) < counts[index]).astype(jnp.float32)
        inputs = centred[rows_of].reshape(slots, N_TP, part_width).astype(jnp.float32)
        w_enc = lax.dynamic_slice_in_dim(enc_weight, index * BLOCK, BLOCK, 1)
        w_enc = w_enc.reshape(N_TP, part_width, BLOCK).astype(jnp.float32)
        parts = jnp.einsum('rtd,tdl->rtl', inputs, w_enc)
        parts = lax.optimization_barrier(parts.astype(jnp.bfloat16)).astype(jnp.float32)
        bias = lax.dynamic_slice_in_dim(enc_bias, index * BLOCK, BLOCK)
        pre = jnp.sum(parts, axis=1) + bias
        latents = jnp.maximum(pre, 0.0).astype(jnp.bfloat16)
        w_dec = lax.dynamic_slice_in_dim(dec_weight, index * BLOCK, BLOCK, 0)
        decoded = jnp.dot(latents, w_dec, preferred_element_type=jnp.float32).astype(jnp.bfloat16)
        decoded = decoded.astype(jnp.float32) * valid[:, None]
        return total.at[rows_of].add(decoded)

    start_total = jnp.zeros(activations.shape, jnp.float32)
    summed = lax.fori_loop(0, N_LAT, one_block, start_total)
    recon = summed + dec_bias
    inputs_full = activations.astype(jnp.float32)
    diff = inputs_full - recon
    token_error = jnp.sum(diff * diff, axis=1) / (jnp.sum(inputs_full * inputs_full, axis=1) + 1e-6)
    mean_error = jnp.sum(token_error) / TOKENS
    return token_error, mean_error
```

```python
import jax
import jax.numpy as jnp
from jax import lax
from jax.sharding import PartitionSpec as P


def score_slots(received, enc_weight, enc_bias, dec_weight):
    owners = received.shape[0]
    slot_count = received.shape[1]
    feature_part = received.shape[2]
    flat_rows = received.reshape(owners * slot_count, feature_part)
    partial_value = jnp.dot(flat_rows, enc_weight, preferred_element_type=jnp.float32)
    pre = lax.psum(partial_value.astype(jnp.bfloat16), "tp").astype(jnp.float32)
    latents = jnp.maximum(pre + enc_bias, 0.0).astype(jnp.bfloat16)
    decoded = jnp.dot(latents, dec_weight, preferred_element_type=jnp.float32).astype(jnp.bfloat16)
    decoded = decoded.reshape(owners, slot_count, feature_part)
    return lax.all_to_all(decoded, "lat", split_axis=0, concat_axis=0, tiled=True)


def finish(activations, summed, dec_bias, owners):
    token_count = activations.shape[0]
    recon = summed + dec_bias
    inputs_full = activations.astype(jnp.float32)
    diff = inputs_full - recon
    squares, norms = lax.psum(
        (jnp.sum(diff * diff, axis=1), jnp.sum(inputs_full * inputs_full, axis=1)), "tp"
    )
    token_error = squares / (norms + 1e-06)
    total = lax.psum(jnp.sum(token_error), "lat")
    mean_error = total / (token_count * owners)
    return (token_error, mean_error)


def general_body(activations, active_blocks, enc_weight, enc_bias, dec_weight, dec_bias):
    owners = lax.axis_size("lat")
    token_count, active_count = active_blocks.shape
    feature_part = activations.shape[1]
    capacity = 2 * token_count * active_count // owners
    centred = (activations.astype(jnp.float32) - dec_bias).astype(jnp.bfloat16)
    flat = active_blocks.reshape(-1)
    onehot = (flat[:, None] == jnp.arange(owners, dtype=jnp.int32)[None, :]).astype(jnp.int32)
    ranks = jnp.sum((jnp.cumsum(onehot, axis=0) - onehot) * onehot, axis=1)
    slot_rows = flat * capacity + ranks
    source_rows = jnp.repeat(centred, active_count, axis=0)
    outgoing = (
        jnp.zeros((owners * capacity, feature_part), jnp.bfloat16).at[slot_rows].set(source_rows)
    )
    outgoing = outgoing.reshape(owners, capacity, feature_part)
    received = lax.all_to_all(outgoing, "lat", split_axis=0, concat_axis=0, tiled=True)
    returned = score_slots(received, enc_weight, enc_bias, dec_weight)
    returned = returned.reshape(owners * capacity, feature_part)
    picked = returned[slot_rows].reshape(token_count, active_count, feature_part)
    return finish(activations, jnp.sum(picked.astype(jnp.float32), axis=1), dec_bias, owners)


def pairs(*hops):
    return [(2 * a + c, 2 * b + c) for a, b in hops for c in range(2)]


TO_INNER = pairs((0, 1), (3, 2))
TO_OUTER = pairs((1, 0), (2, 3))
ACROSS = pairs((1, 2), (2, 1))
COLUMN = [(i, i ^ 1) for i in range(8)]
CORE = [(i, i ^ 1) for i in range(4)]
SIDE = [(i, i ^ 2) for i in range(4)]
OUT_PARTS = 2


def to_inner(x):
    return lax.ppermute(x, "lat", TO_INNER)


def to_outer(x):
    return lax.ppermute(x, "lat", TO_OUTER)


def across(x):
    return lax.ppermute(x, "lat", ACROSS)


def swap_column(x):
    return lax.ppermute(x, "lat", COLUMN)


def line_body(activations, active_blocks, enc_weight, enc_bias, dec_weight, dec_bias):
    owners = 8
    tokens, active_count = active_blocks.shape
    capacity = 2 * tokens * active_count // owners
    width = activations.shape[1]
    block = enc_weight.shape[1]
    half = block // 2
    me = lax.axis_index("lat")
    plane, column = me // 2, me % 2
    inner = (plane == 1) | (plane == 2)
    low = plane < 2
    core = lax.axis_index("tp") % 2

    centred = (activations.astype(jnp.float32) - dec_bias).astype(jnp.bfloat16)
    named_by = lax.all_gather(active_blocks, "lat")

    from_outer = to_inner(centred)
    from_inner = to_outer(centred)
    from_across = across(centred)
    from_inner2 = to_outer(from_across)
    from_across2 = across(from_outer)
    from_inner3 = to_outer(from_across2)
    sources = [
        jnp.where(inner, centred, from_inner),
        jnp.where(inner, from_across, from_inner2),
        jnp.where(inner, from_outer, centred),
        jnp.where(inner, from_across2, from_inner3),
    ]
    near_inner = jnp.where(low, 1, 2)
    near_outer = jnp.where(low, 0, 3)
    order = jnp.stack([near_inner, 3 - near_inner, near_outer, 3 - near_outer])
    blocks_of = named_by[order * 2 + column]
    wanted = jnp.stack([me, me ^ 1])
    named = jnp.any(blocks_of[:, None] == wanted[None, :, None, None], axis=-1)
    earlier = jnp.arange(tokens)[:, None] < jnp.arange(tokens)[None, :]
    ranks = jnp.dot(
        named.reshape(8, tokens).astype(jnp.bfloat16),
        earlier.astype(jnp.bfloat16),
        preferred_element_type=jnp.float32,
    ).astype(jnp.int32).reshape(4, 2, 1, tokens)
    slots = jnp.arange(capacity, dtype=jnp.int32)[None, None, :, None]
    picks = ((ranks == slots) & named[:, :, None, :]).astype(jnp.bfloat16)
    picks = picks.reshape(4, 2 * capacity, tokens)

    bias_half = lax.dynamic_slice_in_dim(enc_bias, core * half, half)

    def pick(first):
        rows = [
            jnp.dot(picks[i], sources[i], preferred_element_type=jnp.float32).astype(jnp.bfloat16)
            for i in (first, first + 1)
        ]
        mine = jnp.concatenate([r[:capacity] for r in rows])
        theirs = jnp.concatenate([r[capacity:] for r in rows])
        return mine, swap_column(theirs)

    def encode(mine, received):
        rows = jnp.concatenate([mine, received])
        part = jnp.dot(rows, enc_weight, preferred_element_type=jnp.float32).astype(jnp.bfloat16)
        left, right = part[:, :half], part[:, half:]
        kept = jnp.where(core == 0, left, right)
        given = jnp.where(core == 0, right, left)
        other = lax.ppermute(given, "tp", CORE)
        chip = (kept.astype(jnp.float32) + other.astype(jnp.float32)).astype(jnp.bfloat16)
        side = lax.ppermute(chip, "tp", SIDE)
        pre = chip.astype(jnp.float32) + side.astype(jnp.float32) + bias_half
        own = jnp.maximum(pre, 0.0).astype(jnp.bfloat16)
        sibling = lax.ppermute(own, "tp", CORE)
        return jnp.concatenate(
            [jnp.where(core == 0, own, sibling), jnp.where(core == 0, sibling, own)], axis=1
        )

    def decode(latents, first, weight):
        decoded = jnp.dot(latents, weight, preferred_element_type=jnp.float32).astype(jnp.bfloat16)
        back = swap_column(decoded[2 * capacity:])
        sums = []
        for i in range(2):
            own = decoded[i * capacity:(i + 1) * capacity]
            other = back[i * capacity:(i + 1) * capacity]
            placed = lax.dot_general(
                picks[first + i],
                jnp.concatenate([own, other]),
                (((0,), (0,)), ((), ())),
                preferred_element_type=jnp.float32,
            )
            sums.append(placed.astype(jnp.bfloat16))
        return sums

    def add(a, b):
        return (a.astype(jnp.float32) + b.astype(jnp.float32)).astype(jnp.bfloat16)

    latents_inner = encode(*pick(0))
    latents_outer = encode(*pick(2))
    summed = []
    step = width // OUT_PARTS
    for p in range(OUT_PARTS):
        weight = dec_weight[:, p * step:(p + 1) * step]
        near, far = decode(latents_inner, 0, weight)
        far1 = to_inner(far)
        far2 = across(add(far, far1))
        near1 = to_inner(near)
        at_inner = near.astype(jnp.float32) + far2.astype(jnp.float32) + near1.astype(jnp.float32)
        own, end = decode(latents_outer, 2, weight)
        end1 = to_inner(end)
        end2 = across(add(end, end1))
        end3 = to_outer(add(own, end2))
        at_outer = own.astype(jnp.float32) + end3.astype(jnp.float32)
        summed.append(jnp.where(inner, at_inner, at_outer))
    return finish(activations, jnp.concatenate(summed, axis=1), dec_bias, owners)


def solution(mesh):
    in_specs = (P("lat", "tp"), P("lat", None), P("tp", "lat"), P("lat"), P("lat", "tp"), P("tp"))
    out_specs = (P("lat"), P())
    body = line_body if (mesh.shape["lat"], mesh.shape["tp"]) == (8, 4) else general_body
    return jax.shard_map(body, mesh=mesh, in_specs=in_specs, out_specs=out_specs, check_vma=False)
```

```python
import functools

import jax
import jax.numpy as jnp
from jax import lax
from jax.experimental import pallas as pl
from jax.experimental.pallas import tpu as pltpu
from jax.sharding import PartitionSpec as P


def score_slots(received, enc_weight, enc_bias, dec_weight):
    owners = received.shape[0]
    slot_count = received.shape[1]
    feature_part = received.shape[2]
    flat_rows = received.reshape(owners * slot_count, feature_part)
    partial_value = jnp.dot(flat_rows, enc_weight, preferred_element_type=jnp.float32)
    pre = lax.psum(partial_value.astype(jnp.bfloat16), "tp").astype(jnp.float32)
    latents = jnp.maximum(pre + enc_bias, 0.0).astype(jnp.bfloat16)
    decoded = jnp.dot(latents, dec_weight, preferred_element_type=jnp.float32).astype(jnp.bfloat16)
    decoded = decoded.reshape(owners, slot_count, feature_part)
    return lax.all_to_all(decoded, "lat", split_axis=0, concat_axis=0, tiled=True)


def finish(activations, summed, dec_bias, owners):
    token_count = activations.shape[0]
    recon = summed + dec_bias
    inputs_full = activations.astype(jnp.float32)
    diff = inputs_full - recon
    squares, norms = lax.psum(
        (jnp.sum(diff * diff, axis=1), jnp.sum(inputs_full * inputs_full, axis=1)), "tp"
    )
    token_error = squares / (norms + 1e-06)
    total = lax.psum(jnp.sum(token_error), "lat")
    mean_error = total / (token_count * owners)
    return (token_error, mean_error)


def general_body(activations, active_blocks, enc_weight, enc_bias, dec_weight, dec_bias):
    owners = lax.axis_size("lat")
    token_count, active_count = active_blocks.shape
    feature_part = activations.shape[1]
    capacity = 2 * token_count * active_count // owners
    centred = (activations.astype(jnp.float32) - dec_bias).astype(jnp.bfloat16)
    flat = active_blocks.reshape(-1)
    onehot = (flat[:, None] == jnp.arange(owners, dtype=jnp.int32)[None, :]).astype(jnp.int32)
    ranks = jnp.sum((jnp.cumsum(onehot, axis=0) - onehot) * onehot, axis=1)
    slot_rows = flat * capacity + ranks
    source_rows = jnp.repeat(centred, active_count, axis=0)
    outgoing = (
        jnp.zeros((owners * capacity, feature_part), jnp.bfloat16).at[slot_rows].set(source_rows)
    )
    outgoing = outgoing.reshape(owners, capacity, feature_part)
    received = lax.all_to_all(outgoing, "lat", split_axis=0, concat_axis=0, tiled=True)
    returned = score_slots(received, enc_weight, enc_bias, dec_weight)
    returned = returned.reshape(owners * capacity, feature_part)
    picked = returned[slot_rows].reshape(token_count, active_count, feature_part)
    return finish(activations, jnp.sum(picked.astype(jnp.float32), axis=1), dec_bias, owners)


MESH = pl.DeviceIdType.MESH
TILE = 256
ROW_PARTS = 4


def line_kernel(
    tokens, capacity,
    act, blocks, enc_hbm, enc_bias, dec_hbm, dec_bias,
    error_out, mean_out,
    enc, dec, src, meta, picks, places, rows, ysend, given, other, kept, chip, side, lat,
    theirs, cat, part, from_mate, from_far, from_end, across2, across3,
    acc, norm, stats, stats_in, mean_own, mean_in,
    w_sem, hop_send, hop_recv, meta_send, meta_recv, pair_send, pair_recv,
    back_send, back_recv, sum_send, sum_recv, end_send, end_recv,
):
    me, tp = lax.axis_index("lat"), lax.axis_index("tp")
    plane, column = me // 2, me % 2
    core = tp % 2
    inner = ((plane + 1) // 2) % 2 == 1
    outer = ((plane + 1) // 2) % 2 == 0
    width = act.shape[1]
    tiles = width // TILE
    half = enc.shape[1] // 2
    part_rows = tokens // ROW_PARTS

    def flip(value, mask):
        for bit in (1, 2, 4):
            if mask & bit:
                value = value + bit - 2 * bit * ((value // bit) % 2)
        return value

    def lat_peer(mask):
        return (flip(me, mask), tp)

    def tp_peer(mask):
        return (me, flip(tp, mask))

    MATE, ACROSS, OPPOSITE, COLUMN = 2, 6, 4, 1

    def remote(src_ref, dst_ref, send, recv, peer):
        return pltpu.make_async_remote_copy(
            src_ref=src_ref, dst_ref=dst_ref, send_sem=send, recv_sem=recv,
            device_id=peer, device_id_type=MESH,
        )

    enc_copy = pltpu.make_async_copy(enc_hbm, enc, w_sem.at[0])
    dec_copy = pltpu.make_async_copy(dec_hbm, dec, w_sem.at[1])
    enc_copy.start()
    dec_copy.start()

    def centre(t, carry):
        cols = pl.ds(pl.multiple_of(t * TILE, TILE), TILE)
        src[0, :, cols] = (act[:, cols].astype(jnp.float32) - dec_bias[:, cols]).astype(jnp.bfloat16)
        return carry

    lax.fori_loop(0, tiles, centre, 0)
    meta[0] = blocks[...]

    barrier = pltpu.get_barrier_semaphore()
    for mask in range(1, 8):
        pl.semaphore_signal(barrier, inc=1, device_id=lat_peer(mask), device_id_type=MESH)
    for mask in range(1, 4):
        pl.semaphore_signal(barrier, inc=1, device_id=tp_peer(mask), device_id_type=MESH)
    pl.semaphore_wait(barrier, 10)

    far_slot = 3 - ((plane + 1) // 2) % 2
    meta_copies = [
        remote(meta.at[0], meta.at[1], meta_send.at[0], meta_recv.at[1], lat_peer(MATE)),
        remote(meta.at[0], meta.at[far_slot], meta_send.at[1], meta_recv.at[far_slot], lat_peer(ACROSS)),
        remote(meta.at[0], meta.at[far_slot], meta_send.at[2], meta_recv.at[far_slot], lat_peer(OPPOSITE)),
    ]
    for copy in meta_copies:
        copy.start()

    flows = [(0, 1, MATE), (0, 2, ACROSS), (2, 2, MATE), (1, 3, ACROSS), (3, 3, MATE)]

    def hop(flow, piece):
        here, there, mask = flows[flow]
        span = pl.ds(pl.multiple_of(piece * part_rows, part_rows), part_rows)
        return remote(
            src.at[here, span], src.at[there, span],
            hop_send.at[flow, piece], hop_recv.at[there, piece], lat_peer(mask),
        )

    def each_piece(fn):
        lax.fori_loop(0, ROW_PARTS, lambda c, carry: (fn(c), carry)[1], 0)

    def each_tile(fn):
        lax.fori_loop(0, tiles, lambda t, carry: (fn(t), carry)[1], 0)

    each_piece(lambda c: hop(0, c).start())

    @pl.when(inner)
    def _():
        each_piece(lambda c: hop(1, c).start())

    def squares_of_inputs(t):
        cols = pl.ds(pl.multiple_of(t * TILE, TILE), TILE)
        value = act[:, cols].astype(jnp.float32)
        norm[...] += value * value

    norm[...] = jnp.zeros_like(norm)
    acc[...] = jnp.zeros_like(acc)
    each_tile(squares_of_inputs)

    earlier = (
        lax.broadcasted_iota(jnp.int32, (tokens, tokens), 0)
        < lax.broadcasted_iota(jnp.int32, (tokens, tokens), 1)
    ).astype(jnp.float32).astype(jnp.bfloat16)
    slots = lax.broadcasted_iota(jnp.int32, (capacity, tokens), 0).astype(jnp.float32)

    def make_picks(k):
        names = meta[k]
        named = []
        for owner in (me, flip(me, COLUMN)):
            hit = jnp.max((names == owner).astype(jnp.float32), axis=0, keepdims=True)
            named.append(jnp.broadcast_to(hit, (8, tokens)))
        named = jnp.concatenate(named)
        ranks = jnp.dot(named.astype(jnp.bfloat16), earlier, preferred_element_type=jnp.float32)
        pick = jnp.concatenate([
            jnp.where(ranks[8 * i:8 * i + 1] == slots, named[8 * i:8 * i + 1], 0.0)
            for i in range(2)
        ])
        picks[k] = pick.astype(jnp.bfloat16)
        places[k] = pick.T.astype(jnp.bfloat16)

    def to_column(k):
        return remote(
            ysend.at[k], rows.at[k, pl.ds(capacity, capacity)],
            pair_send.at[0, k], pair_recv.at[0, k], lat_peer(COLUMN),
        )

    def to_core(k):
        return remote(given.at[k], other.at[k], pair_send.at[1, k], pair_recv.at[1, k], tp_peer(1))

    def to_side(k):
        return remote(chip.at[k], side.at[k], pair_send.at[2, k], pair_recv.at[2, k], tp_peer(2))

    def to_core2(k):
        return remote(
            lat.at[k, core], lat.at[k, core], pair_send.at[3, k], pair_recv.at[3, k], tp_peer(1)
        )

    def pick_rows(k):
        make_picks(k)

        def tile(t):
            cols = pl.ds(pl.multiple_of(t * TILE, TILE), TILE)
            got = jnp.dot(picks[k], src[k, :, cols], preferred_element_type=jnp.float32)
            got = got.astype(jnp.bfloat16)
            rows[k, pl.ds(0, capacity), cols] = got[:capacity]
            ysend[k, :, cols] = got[capacity:]

        each_tile(tile)
        to_column(k).start()

    def encode(k):
        to_column(k).wait_recv()

        def into(target, first):
            def tile(t, carry):
                cols = pl.ds(pl.multiple_of(first + t * TILE, TILE), TILE)
                value = jnp.dot(rows[k], enc[:, cols], preferred_element_type=jnp.float32)
                target(pl.ds(pl.multiple_of(t * TILE, TILE), TILE), value.astype(jnp.bfloat16))
                return carry

            lax.fori_loop(0, half // TILE, tile, 0)

        def set_given(cols, value):
            given[k, :, cols] = value

        def set_kept(cols, value):
            kept[:, cols] = value

        into(set_given, (1 - core) * half)
        to_core(k).start()
        into(set_kept, core * half)
        to_core(k).wait_recv()
        chip[k] = (kept[...].astype(jnp.float32) + other[k].astype(jnp.float32)).astype(jnp.bfloat16)
        to_side(k).start()

    def activate(k):
        to_side(k).wait_recv()
        bias = enc_bias[:, pl.ds(pl.multiple_of(core * half, half), half)]
        pre = chip[k].astype(jnp.float32) + side[k].astype(jnp.float32) + bias
        lat[k, core] = jnp.maximum(pre, 0.0).astype(jnp.bfloat16)
        to_core2(k).start()

    def back(k, t):
        return remote(
            theirs.at[k, t], cat.at[k, t, pl.ds(capacity, capacity)],
            back_send.at[k, t], back_recv.at[k, t], lat_peer(COLUMN),
        )

    def decode(k):
        to_core2(k).wait_recv()

        def tile(t):
            cols = pl.ds(pl.multiple_of(t * TILE, TILE), TILE)
            value = jnp.dot(lat[k, 0], dec[pl.ds(0, half), cols], preferred_element_type=jnp.float32)
            value += jnp.dot(lat[k, 1], dec[pl.ds(half, half), cols], preferred_element_type=jnp.float32)
            value = value.astype(jnp.bfloat16)
            cat[k, t, pl.ds(0, capacity)] = value[:capacity]
            theirs[k, t] = value[capacity:]
            back(k, t).start()

        each_tile(tile)

    sums = [(1, from_mate, MATE), (2, from_far, MATE), (3, from_end, MATE), (2, across2, ACROSS), (3, across3, ACROSS)]

    def pass_on(flow, t):
        k, target, mask = sums[flow]
        return remote(
            part.at[k, t], target.at[t], sum_send.at[flow, t], sum_recv.at[flow, t], lat_peer(mask)
        )

    def add_to_part(k, t, more):
        part[k, t] = (part[k, t].astype(jnp.float32) + more[t].astype(jnp.float32)).astype(jnp.bfloat16)

    def place(k):
        def tile(t):
            back(k, t).wait_recv()
            value = jnp.dot(places[k], cat[k, t], preferred_element_type=jnp.float32)
            part[k, t] = value.astype(jnp.bfloat16)
            if k >= 1:
                @pl.when(outer)
                def _():
                    pass_on(k - 1, t).start()

            if k >= 2:
                @pl.when(inner)
                def _():
                    pass_on(k - 1, t).wait_recv()
                    add_to_part(k, t, (None, None, from_far, from_end)[k])
                    pass_on(k + 1, t).start()

        each_tile(tile)

    def wait_slot(k):
        each_piece(lambda c: hop((0, 0, 1, 3)[k], c).wait_recv())

    meta_done = [
        remote(meta.at[0], meta.at[k], meta_send.at[0], meta_recv.at[k], lat_peer(MATE))
        for k in range(1, 4)
    ]

    pick_rows(0)
    enc_copy.wait()
    encode(0)

    @pl.when(inner)
    def _():
        def forward_far(c):
            hop(1, c).wait_recv()
            hop(2, c).start()

        def forward_mate(c):
            hop(0, c).wait_recv()
            hop(3, c).start()

        each_piece(forward_far)
        each_piece(forward_mate)

    @pl.when(outer)
    def _():
        wait_slot(1)

    meta_done[0].wait_recv()
    pick_rows(1)
    encode(1)
    activate(0)

    @pl.when(outer)
    def _():
        wait_slot(2)

    meta_done[1].wait_recv()
    pick_rows(2)

    @pl.when(inner)
    def _():
        def forward_end(c):
            hop(3, c).wait_recv()
            hop(4, c).start()

        each_piece(forward_end)

    encode(2)
    dec_copy.wait()
    activate(1)
    decode(0)
    decode(1)
    place(0)
    place(1)

    @pl.when(outer)
    def _():
        wait_slot(3)

    meta_done[2].wait_recv()
    pick_rows(3)
    encode(3)
    activate(2)
    decode(2)
    place(2)
    activate(3)
    decode(3)
    place(3)

    @pl.when(inner)
    def _():
        def tile(t):
            pass_on(4, t).wait_recv()
            add_to_part(1, t, across3)
            pass_on(0, t).start()

        each_tile(tile)

    def finish_tile(t):
        pass_on(0, t).wait_recv()
        cols = pl.ds(pl.multiple_of(t * TILE, TILE), TILE)
        diff = act[:, cols].astype(jnp.float32) - dec_bias[:, cols]
        diff = diff - part[0, t].astype(jnp.float32) - from_mate[t].astype(jnp.float32)
        return diff

    @pl.when(outer)
    def _():
        def tile(t):
            diff = finish_tile(t)
            acc[...] += diff * diff

        each_tile(tile)

    @pl.when(inner)
    def _():
        def tile(t):
            pass_on(3, t).wait_recv()
            diff = finish_tile(t) - across2[t].astype(jnp.float32)
            acc[...] += diff * diff

        each_tile(tile)

    stats[0:1] = jnp.sum(acc[...].T, axis=0, keepdims=True)
    stats[1:2] = jnp.sum(norm[...].T, axis=0, keepdims=True)
    stats[2:8] = jnp.zeros((6, tokens), jnp.float32)
    stat_copies = [
        remote(stats, stats_in.at[m], end_send.at[m], end_recv.at[m], tp_peer(m)) for m in range(1, 4)
    ]
    for copy in stat_copies:
        copy.start()
    for copy in stat_copies:
        copy.wait()
    both = (stats[...] + stats_in[1]) + (stats_in[2] + stats_in[3])
    error = both[0:1] / (both[1:2] + 1e-06)
    error_out[...] = jnp.broadcast_to(error, (8, tokens))
    mean_own[...] = jnp.broadcast_to(jnp.sum(error, axis=1, keepdims=True), (8, 128))
    mean_copies = [
        remote(mean_own, mean_in.at[m], end_send.at[3 + m], end_recv.at[3 + m], lat_peer(m))
        for m in range(1, 8)
    ]
    for copy in mean_copies:
        copy.start()
    for copy in mean_copies:
        copy.wait()
    low = (mean_own[...] + mean_in[1]) + (mean_in[2] + mean_in[3])
    high = (mean_in[4] + mean_in[5]) + (mean_in[6] + mean_in[7])
    mean_out[...] = (low + high) / (tokens * 8)

    for copy in meta_copies:
        copy.wait_send()
    each_piece(lambda c: hop(0, c).wait_send())
    for k in range(4):
        for copy in (to_column(k), to_core(k), to_side(k), to_core2(k)):
            copy.wait_send()
        each_tile(lambda t: back(k, t).wait_send())
    each_tile(lambda t: pass_on(0, t).wait_send())

    @pl.when(inner)
    def _():
        for flow in range(1, 5):
            each_piece(lambda c: hop(flow, c).wait_send())
        for flow in (3, 4):
            each_tile(lambda t: pass_on(flow, t).wait_send())

    @pl.when(outer)
    def _():
        for flow in (1, 2):
            each_tile(lambda t: pass_on(flow, t).wait_send())


def line_body(activations, active_blocks, enc_weight, enc_bias, dec_weight, dec_bias):
    tokens, active_count = active_blocks.shape
    capacity = 2 * tokens * active_count // 8
    width = activations.shape[1]
    block = enc_weight.shape[1]
    half = block // 2
    tiles = width // TILE
    names = jnp.pad(active_blocks.T, ((0, 8 - active_count), (0, 0)), constant_values=-1)
    bf, f32 = jnp.bfloat16, jnp.float32
    vm, dma = pltpu.VMEM, pltpu.SemaphoreType.DMA
    in_vmem = pl.BlockSpec(memory_space=pltpu.VMEM)
    anywhere = pl.BlockSpec(memory_space=pl.ANY)
    tiled = (tiles, tokens, TILE)
    error, mean = pl.pallas_call(
        functools.partial(line_kernel, tokens, capacity),
        out_shape=(jax.ShapeDtypeStruct((8, tokens), f32), jax.ShapeDtypeStruct((8, 128), f32)),
        in_specs=[in_vmem, in_vmem, anywhere, in_vmem, anywhere, in_vmem],
        out_specs=(in_vmem, in_vmem),
        scratch_shapes=[
            vm((width, block), bf), vm((block, width), bf),
            vm((4, tokens, width), bf), vm((4, 8, tokens), jnp.int32),
            vm((4, 2 * capacity, tokens), bf), vm((4, tokens, 2 * capacity), bf),
            vm((4, 2 * capacity, width), bf), vm((4, capacity, width), bf),
            vm((4, 2 * capacity, half), bf), vm((4, 2 * capacity, half), bf),
            vm((2 * capacity, half), bf), vm((4, 2 * capacity, half), bf),
            vm((4, 2 * capacity, half), bf), vm((4, 2, 2 * capacity, half), bf),
            vm((4, tiles, capacity, TILE), bf), vm((4, tiles, 2 * capacity, TILE), bf),
            vm((4,) + tiled, bf),
            vm(tiled, bf), vm(tiled, bf), vm(tiled, bf), vm(tiled, bf), vm(tiled, bf),
            vm((tokens, TILE), f32), vm((tokens, TILE), f32),
            vm((8, tokens), f32), vm((4, 8, tokens), f32), vm((8, 128), f32), vm((8, 8, 128), f32),
            dma((2,)), dma((5, ROW_PARTS)), dma((4, ROW_PARTS)), dma((3,)), dma((4,)),
            dma((4, 4)), dma((4, 4)), dma((4, tiles)), dma((4, tiles)),
            dma((5, tiles)), dma((5, tiles)), dma((11,)), dma((11,)),
        ],
        compiler_params=pltpu.CompilerParams(
            collective_id=0, has_side_effects=True, vmem_limit_bytes=60 * 1024 * 1024
        ),
        cost_estimate=pl.CostEstimate(
            flops=4 * 8 * capacity * width * block, bytes_accessed=4 * width * block, transcendentals=0
        ),
    )(activations, names, enc_weight, enc_bias[None], dec_weight, dec_bias[None])
    return error[0], mean[0, 0]


def solution(mesh):
    in_specs = (P("lat", "tp"), P("lat", None), P("tp", "lat"), P("lat"), P("lat", "tp"), P("tp"))
    out_specs = (P("lat"), P())
    body = line_body if (mesh.shape["lat"], mesh.shape["tp"]) == (8, 4) else general_body
    return jax.shard_map(body, mesh=mesh, in_specs=in_specs, out_specs=out_specs, check_vma=False)
```

```python
import functools

import jax
import jax.numpy as jnp
from jax import lax
from jax.experimental import pallas as pl
from jax.experimental.pallas import tpu as pltpu
from jax.sharding import PartitionSpec as P


def score_slots(received, enc_weight, enc_bias, dec_weight):
    owners = received.shape[0]
    slot_count = received.shape[1]
    feature_part = received.shape[2]
    flat_rows = received.reshape(owners * slot_count, feature_part)
    partial_value = jnp.dot(flat_rows, enc_weight, preferred_element_type=jnp.float32)
    pre = lax.psum(partial_value.astype(jnp.bfloat16), "tp").astype(jnp.float32)
    latents = jnp.maximum(pre + enc_bias, 0.0).astype(jnp.bfloat16)
    decoded = jnp.dot(latents, dec_weight, preferred_element_type=jnp.float32).astype(jnp.bfloat16)
    decoded = decoded.reshape(owners, slot_count, feature_part)
    return lax.all_to_all(decoded, "lat", split_axis=0, concat_axis=0, tiled=True)


def finish(activations, summed, dec_bias, owners):
    token_count = activations.shape[0]
    recon = summed + dec_bias
    inputs_full = activations.astype(jnp.float32)
    diff = inputs_full - recon
    squares, norms = lax.psum(
        (jnp.sum(diff * diff, axis=1), jnp.sum(inputs_full * inputs_full, axis=1)), "tp"
    )
    token_error = squares / (norms + 1e-06)
    total = lax.psum(jnp.sum(token_error), "lat")
    mean_error = total / (token_count * owners)
    return (token_error, mean_error)


def general_body(activations, active_blocks, enc_weight, enc_bias, dec_weight, dec_bias):
    owners = lax.axis_size("lat")
    token_count, active_count = active_blocks.shape
    feature_part = activations.shape[1]
    capacity = 2 * token_count * active_count // owners
    centred = (activations.astype(jnp.float32) - dec_bias).astype(jnp.bfloat16)
    flat = active_blocks.reshape(-1)
    onehot = (flat[:, None] == jnp.arange(owners, dtype=jnp.int32)[None, :]).astype(jnp.int32)
    ranks = jnp.sum((jnp.cumsum(onehot, axis=0) - onehot) * onehot, axis=1)
    slot_rows = flat * capacity + ranks
    source_rows = jnp.repeat(centred, active_count, axis=0)
    outgoing = (
        jnp.zeros((owners * capacity, feature_part), jnp.bfloat16).at[slot_rows].set(source_rows)
    )
    outgoing = outgoing.reshape(owners, capacity, feature_part)
    received = lax.all_to_all(outgoing, "lat", split_axis=0, concat_axis=0, tiled=True)
    returned = score_slots(received, enc_weight, enc_bias, dec_weight)
    returned = returned.reshape(owners * capacity, feature_part)
    picked = returned[slot_rows].reshape(token_count, active_count, feature_part)
    return finish(activations, jnp.sum(picked.astype(jnp.float32), axis=1), dec_bias, owners)


MESH = pl.DeviceIdType.MESH
TILE = 256


def line_kernel(
    tokens, capacity,
    act, blocks, enc_hbm, enc_bias, dec_hbm, dec_bias,
    error_out, mean_out,
    enc, dec, src, meta, picks, places, rows, ysend, given, other, chip, side, lat,
    theirs, cat, part, from_mate, from_far, from_end, across2, across3,
    acc, norm, stats, stats_in, mean_own, mean_in,
    w_sem, hop_send, hop_recv, meta_send, meta_recv, col_send, col_recv, pair_send, pair_recv,
    back_send, back_recv, sum_send, sum_recv, end_send, end_recv,
):
    me, tp = lax.axis_index("lat"), lax.axis_index("tp")
    plane, column = me // 2, me % 2
    core = tp % 2
    inner = ((plane + 1) // 2) % 2 == 1
    outer = ((plane + 1) // 2) % 2 == 0
    width = act.shape[1]
    tiles = width // TILE
    half = enc.shape[1] // 2
    half_tiles = half // TILE

    def flip(value, mask):
        for bit in (1, 2, 4):
            if mask & bit:
                value = value + bit - 2 * bit * ((value // bit) % 2)
        return value

    def lat_peer(mask):
        return (flip(me, mask), tp)

    def tp_peer(mask):
        return (me, flip(tp, mask))

    MATE, ACROSS, OPPOSITE, COLUMN = 2, 6, 4, 1

    def columns(t, first=0):
        return pl.ds(pl.multiple_of(first + t * TILE, TILE), TILE)

    def remote(src_ref, dst_ref, send, recv, peer):
        return pltpu.make_async_remote_copy(
            src_ref=src_ref, dst_ref=dst_ref, send_sem=send, recv_sem=recv,
            device_id=peer, device_id_type=MESH,
        )

    enc_copy = pltpu.make_async_copy(enc_hbm, enc, w_sem.at[0])
    dec_copy = pltpu.make_async_copy(dec_hbm, dec, w_sem.at[1])
    enc_copy.start()
    dec_copy.start()

    def centre(t, carry):
        cols = pl.ds(pl.multiple_of(t * TILE, TILE), TILE)
        src[0, :, cols] = (act[:, cols].astype(jnp.float32) - dec_bias[:, cols]).astype(jnp.bfloat16)
        return carry

    lax.fori_loop(0, tiles, centre, 0)
    meta[0] = blocks[...]

    barrier = pltpu.get_barrier_semaphore()
    for mask in range(1, 8):
        pl.semaphore_signal(barrier, inc=1, device_id=lat_peer(mask), device_id_type=MESH)
    for mask in range(1, 4):
        pl.semaphore_signal(barrier, inc=1, device_id=tp_peer(mask), device_id_type=MESH)
    pl.semaphore_wait(barrier, 10)

    far_slot = 3 - ((plane + 1) // 2) % 2
    meta_copies = [
        remote(meta.at[0], meta.at[1], meta_send.at[0], meta_recv.at[1], lat_peer(MATE)),
        remote(meta.at[0], meta.at[far_slot], meta_send.at[1], meta_recv.at[far_slot], lat_peer(ACROSS)),
        remote(meta.at[0], meta.at[far_slot], meta_send.at[2], meta_recv.at[far_slot], lat_peer(OPPOSITE)),
    ]
    for copy in meta_copies:
        copy.start()

    flows = [(0, 1, MATE), (0, 2, ACROSS), (2, 2, MATE), (1, 3, ACROSS), (3, 3, MATE)]

    def hop(flow, piece):
        here, there, mask = flows[flow]
        return remote(
            src.at[here, :, columns(piece)], src.at[there, :, columns(piece)],
            hop_send.at[flow, piece], hop_recv.at[there, piece], lat_peer(mask),
        )

    def each_tile(fn):
        lax.fori_loop(0, tiles, lambda t, carry: (fn(t), carry)[1], 0)

    def each_half_tile(fn):
        lax.fori_loop(0, half_tiles, lambda t, carry: (fn(t), carry)[1], 0)

    each_tile(lambda t: hop(0, t).start())

    @pl.when(inner)
    def _():
        each_tile(lambda t: hop(1, t).start())

    def squares_of_inputs(t):
        cols = pl.ds(pl.multiple_of(t * TILE, TILE), TILE)
        value = act[:, cols].astype(jnp.float32)
        norm[...] += value * value

    norm[...] = jnp.zeros_like(norm)
    acc[...] = jnp.zeros_like(acc)
    each_tile(squares_of_inputs)

    earlier = (
        lax.broadcasted_iota(jnp.int32, (tokens, tokens), 0)
        < lax.broadcasted_iota(jnp.int32, (tokens, tokens), 1)
    ).astype(jnp.float32).astype(jnp.bfloat16)
    slots = lax.broadcasted_iota(jnp.int32, (capacity, tokens), 0).astype(jnp.float32)

    def make_picks(k):
        names = meta[k]
        named = []
        for owner in (me, flip(me, COLUMN)):
            hit = jnp.max((names == owner).astype(jnp.float32), axis=0, keepdims=True)
            named.append(jnp.broadcast_to(hit, (8, tokens)))
        named = jnp.concatenate(named)
        ranks = jnp.dot(named.astype(jnp.bfloat16), earlier, preferred_element_type=jnp.float32)
        pick = jnp.concatenate([
            jnp.where(ranks[8 * i:8 * i + 1] == slots, named[8 * i:8 * i + 1], 0.0)
            for i in range(2)
        ])
        picks[k] = pick.astype(jnp.bfloat16)
        places[k] = pick.T.astype(jnp.bfloat16)

    def to_column(k, t):
        return remote(
            ysend.at[k, :, columns(t)], rows.at[k, pl.ds(capacity, capacity), columns(t)],
            col_send.at[k, t], col_recv.at[k, t], lat_peer(COLUMN),
        )

    def to_core(k, t):
        return remote(
            given.at[k, :, columns(t)], other.at[k, :, columns(t)],
            pair_send.at[0, k, t], pair_recv.at[0, k, t], tp_peer(1),
        )

    def to_side(k, t):
        return remote(
            chip.at[k, :, columns(t)], side.at[k, :, columns(t)],
            pair_send.at[1, k, t], pair_recv.at[1, k, t], tp_peer(2),
        )

    def to_core2(k, t):
        return remote(
            lat.at[k, core, :, columns(t)], lat.at[k, core, :, columns(t)],
            pair_send.at[2, k, t], pair_recv.at[2, k, t], tp_peer(1),
        )

    def pick_tile(k, t):
        got = jnp.dot(picks[k], src[k, :, columns(t)], preferred_element_type=jnp.float32)
        got = got.astype(jnp.bfloat16)
        rows[k, pl.ds(0, capacity), columns(t)] = got[:capacity]
        ysend[k, :, columns(t)] = got[capacity:]
        to_column(k, t).start()

    def encode(k):
        each_tile(lambda t: to_column(k, t).wait_recv())

        def give(t):
            cols = columns(t, (1 - core) * half)
            value = jnp.dot(rows[k], enc[:, cols], preferred_element_type=jnp.float32)
            given[k, :, columns(t)] = value.astype(jnp.bfloat16)
            to_core(k, t).start()

        def keep(t):
            cols = columns(t, core * half)
            value = jnp.dot(rows[k], enc[:, cols], preferred_element_type=jnp.float32)
            to_core(k, t).wait_recv()
            value += other[k, :, columns(t)].astype(jnp.float32)
            chip[k, :, columns(t)] = value.astype(jnp.bfloat16)
            to_side(k, t).start()

        each_half_tile(give)
        each_half_tile(keep)

    def activate(k):
        def tile(t):
            to_side(k, t).wait_recv()
            bias = enc_bias[:, columns(t, core * half)]
            pre = chip[k, :, columns(t)].astype(jnp.float32) + side[k, :, columns(t)].astype(jnp.float32)
            lat[k, core, :, columns(t)] = jnp.maximum(pre + bias, 0.0).astype(jnp.bfloat16)
            to_core2(k, t).start()

        each_half_tile(tile)

    def back(k, t):
        return remote(
            theirs.at[k, t], cat.at[k, t, pl.ds(capacity, capacity)],
            back_send.at[k, t], back_recv.at[k, t], lat_peer(COLUMN),
        )

    def decode(k):
        each_half_tile(lambda t: to_core2(k, t).wait_recv())

        def tile(t):
            cols = pl.ds(pl.multiple_of(t * TILE, TILE), TILE)
            value = jnp.dot(lat[k, 0], dec[pl.ds(0, half), cols], preferred_element_type=jnp.float32)
            value += jnp.dot(lat[k, 1], dec[pl.ds(half, half), cols], preferred_element_type=jnp.float32)
            value = value.astype(jnp.bfloat16)
            cat[k, t, pl.ds(0, capacity)] = value[:capacity]
            theirs[k, t] = value[capacity:]
            back(k, t).start()

        each_tile(tile)

    sums = [(1, from_mate, MATE), (2, from_far, MATE), (3, from_end, MATE), (2, across2, ACROSS), (3, across3, ACROSS)]

    def pass_on(flow, t):
        k, target, mask = sums[flow]
        return remote(
            part.at[k, t], target.at[t], sum_send.at[flow, t], sum_recv.at[flow, t], lat_peer(mask)
        )

    def add_to_part(k, t, more):
        part[k, t] = (part[k, t].astype(jnp.float32) + more[t].astype(jnp.float32)).astype(jnp.bfloat16)

    def place_tile(k, t):
        back(k, t).wait_recv()
        value = jnp.dot(places[k], cat[k, t], preferred_element_type=jnp.float32)
        part[k, t] = value.astype(jnp.bfloat16)
        if k >= 1:
            @pl.when(outer)
            def _():
                pass_on(k - 1, t).start()

    def place(k):
        each_tile(lambda t: place_tile(k, t))

    meta_done = [
        remote(meta.at[0], meta.at[k], meta_send.at[0], meta_recv.at[k], lat_peer(MATE))
        for k in range(1, 4)
    ]

    make_picks(0)
    each_tile(lambda t: pick_tile(0, t))
    for k in range(1, 4):
        meta_done[k - 1].wait_recv()
        make_picks(k)

    @pl.when(inner)
    def _():
        def tile(t):
            hop(1, t).wait_recv()
            hop(2, t).start()
            hop(0, t).wait_recv()
            hop(3, t).start()
            pick_tile(1, t)

        each_tile(tile)

    @pl.when(outer)
    def _():
        def tile(t):
            hop(0, t).wait_recv()
            pick_tile(1, t)

        each_tile(tile)

    enc_copy.wait()
    encode(0)
    encode(1)

    @pl.when(inner)
    def _():
        def tile(t):
            hop(3, t).wait_recv()
            hop(4, t).start()
            pick_tile(3, t)

        each_tile(lambda t: pick_tile(2, t))
        each_tile(tile)

    @pl.when(outer)
    def _():
        def tile(t):
            hop(2, t).wait_recv()
            pick_tile(2, t)

        each_tile(tile)

    activate(0)
    encode(2)
    activate(1)
    dec_copy.wait()
    decode(0)
    decode(1)

    @pl.when(outer)
    def _():
        def tile(t):
            hop(3, t).wait_recv()
            pick_tile(3, t)

        each_tile(tile)

    encode(3)
    activate(2)
    decode(2)
    place(1)
    place(2)
    activate(3)
    decode(3)
    place(0)

    @pl.when(outer)
    def _():
        place(3)

    @pl.when(inner)
    def _():
        def far_tile(t):
            pass_on(1, t).wait_recv()
            add_to_part(2, t, from_far)
            pass_on(3, t).start()

        def last_hop(t):
            pass_on(4, t).wait_recv()
            add_to_part(1, t, across3)
            pass_on(0, t).start()

        def end_tile(t):
            place_tile(3, t)
            pass_on(2, t).wait_recv()
            add_to_part(3, t, from_end)
            pass_on(4, t).start()

            @pl.when(t >= 1)
            def _():
                last_hop(t - 1)

        each_tile(far_tile)
        each_tile(end_tile)
        last_hop(tiles - 1)

    def finish_tile(t):
        pass_on(0, t).wait_recv()
        cols = pl.ds(pl.multiple_of(t * TILE, TILE), TILE)
        diff = act[:, cols].astype(jnp.float32) - dec_bias[:, cols]
        diff = diff - part[0, t].astype(jnp.float32) - from_mate[t].astype(jnp.float32)
        return diff

    @pl.when(outer)
    def _():
        def tile(t):
            diff = finish_tile(t)
            acc[...] += diff * diff

        each_tile(tile)

    @pl.when(inner)
    def _():
        def tile(t):
            pass_on(3, t).wait_recv()
            diff = finish_tile(t) - across2[t].astype(jnp.float32)
            acc[...] += diff * diff

        each_tile(tile)

    stats[0:1] = jnp.sum(acc[...].T, axis=0, keepdims=True)
    stats[1:2] = jnp.sum(norm[...].T, axis=0, keepdims=True)
    stats[2:8] = jnp.zeros((6, tokens), jnp.float32)
    stat_copies = [
        remote(stats, stats_in.at[m], end_send.at[m], end_recv.at[m], tp_peer(m)) for m in range(1, 4)
    ]
    for copy in stat_copies:
        copy.start()
    for copy in stat_copies:
        copy.wait()
    both = (stats[...] + stats_in[1]) + (stats_in[2] + stats_in[3])
    error = both[0:1] / (both[1:2] + 1e-06)
    error_out[...] = jnp.broadcast_to(error, (8, tokens))
    mean_own[...] = jnp.broadcast_to(jnp.sum(error, axis=1, keepdims=True), (8, 128))
    mean_copies = [
        remote(mean_own, mean_in.at[m], end_send.at[3 + m], end_recv.at[3 + m], lat_peer(m))
        for m in range(1, 8)
    ]
    for copy in mean_copies:
        copy.start()
    for copy in mean_copies:
        copy.wait()
    low = (mean_own[...] + mean_in[1]) + (mean_in[2] + mean_in[3])
    high = (mean_in[4] + mean_in[5]) + (mean_in[6] + mean_in[7])
    mean_out[...] = (low + high) / (tokens * 8)

    for copy in meta_copies:
        copy.wait_send()
    each_tile(lambda t: hop(0, t).wait_send())
    for k in range(4):
        each_tile(lambda t: to_column(k, t).wait_send())
        for flow in (to_core, to_side, to_core2):
            each_half_tile(lambda t: flow(k, t).wait_send())
        each_tile(lambda t: back(k, t).wait_send())
    each_tile(lambda t: pass_on(0, t).wait_send())

    @pl.when(inner)
    def _():
        for flow in range(1, 5):
            each_tile(lambda t: hop(flow, t).wait_send())
        for flow in (3, 4):
            each_tile(lambda t: pass_on(flow, t).wait_send())

    @pl.when(outer)
    def _():
        for flow in (1, 2):
            each_tile(lambda t: pass_on(flow, t).wait_send())


def line_body(activations, active_blocks, enc_weight, enc_bias, dec_weight, dec_bias):
    tokens, active_count = active_blocks.shape
    capacity = 2 * tokens * active_count // 8
    width = activations.shape[1]
    block = enc_weight.shape[1]
    half = block // 2
    tiles = width // TILE
    names = jnp.pad(active_blocks.T, ((0, 8 - active_count), (0, 0)), constant_values=-1)
    bf, f32 = jnp.bfloat16, jnp.float32
    vm, dma = pltpu.VMEM, pltpu.SemaphoreType.DMA
    in_vmem = pl.BlockSpec(memory_space=pltpu.VMEM)
    anywhere = pl.BlockSpec(memory_space=pl.ANY)
    tiled = (tiles, tokens, TILE)
    error, mean = pl.pallas_call(
        functools.partial(line_kernel, tokens, capacity),
        out_shape=(jax.ShapeDtypeStruct((8, tokens), f32), jax.ShapeDtypeStruct((8, 128), f32)),
        in_specs=[in_vmem, in_vmem, anywhere, in_vmem, anywhere, in_vmem],
        out_specs=(in_vmem, in_vmem),
        scratch_shapes=[
            vm((width, block), bf), vm((block, width), bf),
            vm((4, tokens, width), bf), vm((4, 8, tokens), jnp.int32),
            vm((4, 2 * capacity, tokens), bf), vm((4, tokens, 2 * capacity), bf),
            vm((4, 2 * capacity, width), bf), vm((4, capacity, width), bf),
            vm((4, 2 * capacity, half), bf), vm((4, 2 * capacity, half), bf),
            vm((4, 2 * capacity, half), bf), vm((4, 2 * capacity, half), bf),
            vm((4, 2, 2 * capacity, half), bf),
            vm((4, tiles, capacity, TILE), bf), vm((4, tiles, 2 * capacity, TILE), bf),
            vm((4,) + tiled, bf),
            vm(tiled, bf), vm(tiled, bf), vm(tiled, bf), vm(tiled, bf), vm(tiled, bf),
            vm((tokens, TILE), f32), vm((tokens, TILE), f32),
            vm((8, tokens), f32), vm((4, 8, tokens), f32), vm((8, 128), f32), vm((8, 8, 128), f32),
            dma((2,)), dma((5, tiles)), dma((4, tiles)), dma((3,)), dma((4,)),
            dma((4, tiles)), dma((4, tiles)), dma((3, 4, half // TILE)), dma((3, 4, half // TILE)),
            dma((4, tiles)), dma((4, tiles)),
            dma((5, tiles)), dma((5, tiles)), dma((11,)), dma((11,)),
        ],
        compiler_params=pltpu.CompilerParams(
            collective_id=0, has_side_effects=True, vmem_limit_bytes=60 * 1024 * 1024
        ),
        cost_estimate=pl.CostEstimate(
            flops=4 * 8 * capacity * width * block, bytes_accessed=4 * width * block, transcendentals=0
        ),
    )(activations, names, enc_weight, enc_bias[None], dec_weight, dec_bias[None])
    return error[0], mean[0, 0]


def solution(mesh):
    in_specs = (P("lat", "tp"), P("lat", None), P("tp", "lat"), P("lat"), P("lat", "tp"), P("tp"))
    out_specs = (P("lat"), P())
    body = line_body if (mesh.shape["lat"], mesh.shape["tp"]) == (8, 4) else general_body
    return jax.shard_map(body, mesh=mesh, in_specs=in_specs, out_specs=out_specs, check_vma=False)
```

```python
import functools

import jax
import jax.numpy as jnp
from jax import lax
from jax.experimental import pallas as pl
from jax.experimental.pallas import tpu as pltpu
from jax.sharding import PartitionSpec as P


def score_slots(received, enc_weight, enc_bias, dec_weight):
    owners = received.shape[0]
    slot_count = received.shape[1]
    feature_part = received.shape[2]
    flat_rows = received.reshape(owners * slot_count, feature_part)
    partial_value = jnp.dot(flat_rows, enc_weight, preferred_element_type=jnp.float32)
    pre = lax.psum(partial_value.astype(jnp.bfloat16), "tp").astype(jnp.float32)
    latents = jnp.maximum(pre + enc_bias, 0.0).astype(jnp.bfloat16)
    decoded = jnp.dot(latents, dec_weight, preferred_element_type=jnp.float32).astype(jnp.bfloat16)
    decoded = decoded.reshape(owners, slot_count, feature_part)
    return lax.all_to_all(decoded, "lat", split_axis=0, concat_axis=0, tiled=True)


def finish(activations, summed, dec_bias, owners):
    token_count = activations.shape[0]
    recon = summed + dec_bias
    inputs_full = activations.astype(jnp.float32)
    diff = inputs_full - recon
    squares, norms = lax.psum(
        (jnp.sum(diff * diff, axis=1), jnp.sum(inputs_full * inputs_full, axis=1)), "tp"
    )
    token_error = squares / (norms + 1e-06)
    total = lax.psum(jnp.sum(token_error), "lat")
    mean_error = total / (token_count * owners)
    return (token_error, mean_error)


def general_body(activations, active_blocks, enc_weight, enc_bias, dec_weight, dec_bias):
    owners = lax.axis_size("lat")
    token_count, active_count = active_blocks.shape
    feature_part = activations.shape[1]
    capacity = 2 * token_count * active_count // owners
    centred = (activations.astype(jnp.float32) - dec_bias).astype(jnp.bfloat16)
    flat = active_blocks.reshape(-1)
    onehot = (flat[:, None] == jnp.arange(owners, dtype=jnp.int32)[None, :]).astype(jnp.int32)
    ranks = jnp.sum((jnp.cumsum(onehot, axis=0) - onehot) * onehot, axis=1)
    slot_rows = flat * capacity + ranks
    source_rows = jnp.repeat(centred, active_count, axis=0)
    outgoing = (
        jnp.zeros((owners * capacity, feature_part), jnp.bfloat16).at[slot_rows].set(source_rows)
    )
    outgoing = outgoing.reshape(owners, capacity, feature_part)
    received = lax.all_to_all(outgoing, "lat", split_axis=0, concat_axis=0, tiled=True)
    returned = score_slots(received, enc_weight, enc_bias, dec_weight)
    returned = returned.reshape(owners * capacity, feature_part)
    picked = returned[slot_rows].reshape(token_count, active_count, feature_part)
    return finish(activations, jnp.sum(picked.astype(jnp.float32), axis=1), dec_bias, owners)


MESH = pl.DeviceIdType.MESH
TILE = 256


def line_kernel(
    tokens, capacity,
    act, blocks, enc_hbm, enc_bias, dec_hbm, dec_bias,
    error_out, mean_out,
    enc, dec, src, meta, picks, places, rows, ysend, given, other, chip, side, lat,
    theirs, cat, part, from_mate, from_far, from_end, across2, across3,
    acc, norm, stats, stats_in, mean_own, mean_in,
    w_sem, hop_send, hop_recv, meta_send, meta_recv, col_send, col_recv, pair_send, pair_recv,
    back_send, back_recv, sum_send, sum_recv, end_send, end_recv,
):
    me, tp = lax.axis_index("lat"), lax.axis_index("tp")
    plane, column = me // 2, me % 2
    core = tp % 2
    inner = ((plane + 1) // 2) % 2 == 1
    outer = ((plane + 1) // 2) % 2 == 0
    width = act.shape[1]
    tiles = width // TILE
    half = enc.shape[1] // 2
    half_tiles = half // TILE

    def flip(value, mask):
        for bit in (1, 2, 4):
            if mask & bit:
                value = value + bit - 2 * bit * ((value // bit) % 2)
        return value

    def lat_peer(mask):
        return (flip(me, mask), tp)

    def tp_peer(mask):
        return (me, flip(tp, mask))

    MATE, ACROSS, OPPOSITE, COLUMN = 2, 6, 4, 1

    def columns(t, first=0):
        return pl.ds(pl.multiple_of(first + t * TILE, TILE), TILE)

    def remote(src_ref, dst_ref, send, recv, peer):
        return pltpu.make_async_remote_copy(
            src_ref=src_ref, dst_ref=dst_ref, send_sem=send, recv_sem=recv,
            device_id=peer, device_id_type=MESH,
        )

    enc_copy = pltpu.make_async_copy(enc_hbm, enc, w_sem.at[0])
    dec_copy = pltpu.make_async_copy(dec_hbm, dec, w_sem.at[1])
    enc_copy.start()
    dec_copy.start()

    def centre(t, carry):
        cols = pl.ds(pl.multiple_of(t * TILE, TILE), TILE)
        src[0, :, cols] = (act[:, cols].astype(jnp.float32) - dec_bias[:, cols]).astype(jnp.bfloat16)
        return carry

    lax.fori_loop(0, tiles, centre, 0)
    meta[0] = blocks[...]

    barrier = pltpu.get_barrier_semaphore()
    for mask in range(1, 8):
        pl.semaphore_signal(barrier, inc=1, device_id=lat_peer(mask), device_id_type=MESH)
    for mask in range(1, 4):
        pl.semaphore_signal(barrier, inc=1, device_id=tp_peer(mask), device_id_type=MESH)
    pl.semaphore_wait(barrier, 10)

    far_slot = 3 - ((plane + 1) // 2) % 2
    meta_copies = [
        remote(meta.at[0], meta.at[1], meta_send.at[0], meta_recv.at[1], lat_peer(MATE)),
        remote(meta.at[0], meta.at[far_slot], meta_send.at[1], meta_recv.at[far_slot], lat_peer(ACROSS)),
        remote(meta.at[0], meta.at[far_slot], meta_send.at[2], meta_recv.at[far_slot], lat_peer(OPPOSITE)),
    ]
    for copy in meta_copies:
        copy.start()

    flows = [(0, 1, MATE), (0, 2, ACROSS), (2, 2, MATE), (1, 3, ACROSS), (3, 3, MATE)]

    def hop(flow, piece):
        here, there, mask = flows[flow]
        return remote(
            src.at[here, :, columns(piece)], src.at[there, :, columns(piece)],
            hop_send.at[flow, piece], hop_recv.at[there, piece], lat_peer(mask),
        )

    def each_tile(fn, first=0, last=tiles):
        lax.fori_loop(first, last, lambda t, carry: (fn(t), carry)[1], 0)

    def each_half_tile(fn):
        lax.fori_loop(0, half_tiles, lambda t, carry: (fn(t), carry)[1], 0)

    def first_hops(t):
        hop(0, t).start()

        @pl.when(inner)
        def _():
            hop(1, t).start()

    each_tile(first_hops)

    def squares_of_inputs(t):
        cols = pl.ds(pl.multiple_of(t * TILE, TILE), TILE)
        value = act[:, cols].astype(jnp.float32)
        norm[...] += value * value

    norm[...] = jnp.zeros_like(norm)
    acc[...] = jnp.zeros_like(acc)
    each_tile(squares_of_inputs)

    earlier = (
        lax.broadcasted_iota(jnp.int32, (tokens, tokens), 0)
        < lax.broadcasted_iota(jnp.int32, (tokens, tokens), 1)
    ).astype(jnp.float32).astype(jnp.bfloat16)
    slots = lax.broadcasted_iota(jnp.int32, (capacity, tokens), 0).astype(jnp.float32)

    def make_picks(k):
        names = meta[k]
        named = []
        for owner in (me, flip(me, COLUMN)):
            hit = jnp.max((names == owner).astype(jnp.float32), axis=0, keepdims=True)
            named.append(jnp.broadcast_to(hit, (8, tokens)))
        named = jnp.concatenate(named)
        ranks = jnp.dot(named.astype(jnp.bfloat16), earlier, preferred_element_type=jnp.float32)
        pick = jnp.concatenate([
            jnp.where(ranks[8 * i:8 * i + 1] == slots, named[8 * i:8 * i + 1], 0.0)
            for i in range(2)
        ])
        picks[k] = pick.astype(jnp.bfloat16)
        places[k] = pick.T.astype(jnp.bfloat16)

    def to_column(k, t):
        return remote(
            ysend.at[k, :, columns(t)], rows.at[k, pl.ds(capacity, capacity), columns(t)],
            col_send.at[k, t], col_recv.at[k, t], lat_peer(COLUMN),
        )

    def to_core(k, t):
        return remote(
            given.at[k, :, columns(t)], other.at[k, :, columns(t)],
            pair_send.at[0, k, t], pair_recv.at[0, k, t], tp_peer(1),
        )

    def to_side(k, t):
        return remote(
            chip.at[k, :, columns(t)], side.at[k, :, columns(t)],
            pair_send.at[1, k, t], pair_recv.at[1, k, t], tp_peer(2),
        )

    def to_core2(k, t):
        return remote(
            lat.at[k, core, :, columns(t)], lat.at[k, core, :, columns(t)],
            pair_send.at[2, k, t], pair_recv.at[2, k, t], tp_peer(1),
        )

    def pick_tile(k, t):
        got = jnp.dot(picks[k], src[k, :, columns(t)], preferred_element_type=jnp.float32)
        got = got.astype(jnp.bfloat16)
        rows[k, pl.ds(0, capacity), columns(t)] = got[:capacity]
        ysend[k, :, columns(t)] = got[capacity:]
        to_column(k, t).start()

    def encode(k):
        each_tile(lambda t: to_column(k, t).wait_recv())

        def give(t):
            cols = columns(t, (1 - core) * half)
            value = jnp.dot(rows[k], enc[:, cols], preferred_element_type=jnp.float32)
            given[k, :, columns(t)] = value.astype(jnp.bfloat16)
            to_core(k, t).start()

        def keep(t):
            cols = columns(t, core * half)
            value = jnp.dot(rows[k], enc[:, cols], preferred_element_type=jnp.float32)
            to_core(k, t).wait_recv()
            value += other[k, :, columns(t)].astype(jnp.float32)
            chip[k, :, columns(t)] = value.astype(jnp.bfloat16)
            to_side(k, t).start()

        each_half_tile(give)
        each_half_tile(keep)

    def activate(k):
        def tile(t):
            to_side(k, t).wait_recv()
            bias = enc_bias[:, columns(t, core * half)]
            pre = chip[k, :, columns(t)].astype(jnp.float32) + side[k, :, columns(t)].astype(jnp.float32)
            lat[k, core, :, columns(t)] = jnp.maximum(pre + bias, 0.0).astype(jnp.bfloat16)
            to_core2(k, t).start()

        each_half_tile(tile)

    def back(k, t):
        return remote(
            theirs.at[k, t], cat.at[k, t, pl.ds(capacity, capacity)],
            back_send.at[k, t], back_recv.at[k, t], lat_peer(COLUMN),
        )

    def wait_latents(k):
        each_half_tile(lambda t: to_core2(k, t).wait_recv())

    def decode_tile(k, t):
        cols = columns(t)
        value = jnp.dot(lat[k, 0], dec[pl.ds(0, half), cols], preferred_element_type=jnp.float32)
        value += jnp.dot(lat[k, 1], dec[pl.ds(half, half), cols], preferred_element_type=jnp.float32)
        value = value.astype(jnp.bfloat16)
        cat[k, t, pl.ds(0, capacity)] = value[:capacity]
        theirs[k, t] = value[capacity:]
        back(k, t).start()

    sums = [(1, from_mate, MATE), (2, from_far, MATE), (3, from_end, MATE), (2, across2, ACROSS), (3, across3, ACROSS)]

    def pass_on(flow, t):
        k, target, mask = sums[flow]
        return remote(
            part.at[k, t], target.at[t], sum_send.at[flow, t], sum_recv.at[flow, t], lat_peer(mask)
        )

    def add_to_part(k, t, more):
        part[k, t] = (part[k, t].astype(jnp.float32) + more[t].astype(jnp.float32)).astype(jnp.bfloat16)

    def place_tile(k, t):
        back(k, t).wait_recv()
        value = jnp.dot(places[k], cat[k, t], preferred_element_type=jnp.float32)
        part[k, t] = value.astype(jnp.bfloat16)
        if k >= 1:
            @pl.when(outer)
            def _():
                pass_on(k - 1, t).start()

    LAG = 3

    def place_behind(k, t):
        @pl.when(t >= LAG)
        def _():
            place_tile(k, t - LAG)

    def place_rest(k):
        each_tile(lambda t: place_tile(k, t), tiles - LAG)

    meta_done = [
        remote(meta.at[0], meta.at[k], meta_send.at[0], meta_recv.at[k], lat_peer(MATE))
        for k in range(1, 4)
    ]

    make_picks(0)
    each_tile(lambda t: pick_tile(0, t))
    for k in range(1, 4):
        meta_done[k - 1].wait_recv()
        make_picks(k)

    def mate_arrives(t):
        @pl.when(inner)
        def _():
            hop(1, t).wait_recv()
            hop(2, t).start()

        hop(0, t).wait_recv()

        @pl.when(inner)
        def _():
            hop(3, t).start()

        pick_tile(1, t)

    def far_inner_arrives(t):
        @pl.when(outer)
        def _():
            hop(2, t).wait_recv()

        @pl.when(inner)
        def _():
            hop(3, t).wait_recv()
            hop(4, t).start()

        pick_tile(2, t)
        decode_tile(0, t)

    def far_outer_arrives(t):
        @pl.when(outer)
        def _():
            hop(3, t).wait_recv()

        pick_tile(3, t)
        decode_tile(1, t)
        place_behind(1, t)

    def third_decode(t):
        decode_tile(2, t)
        place_behind(2, t)
        place_tile(0, t)

    def last_decode(t):
        decode_tile(3, t)

        @pl.when(outer)
        def _():
            place_behind(3, t)

    each_tile(mate_arrives, 0, tiles // 2)
    enc_copy.wait()
    encode(0)
    each_tile(mate_arrives, tiles // 2, tiles)
    encode(1)
    activate(0)
    dec_copy.wait()
    wait_latents(0)
    each_tile(far_inner_arrives)
    activate(1)
    encode(2)
    wait_latents(1)
    each_tile(far_outer_arrives)
    activate(2)
    place_rest(1)
    encode(3)
    wait_latents(2)
    each_tile(third_decode)
    place_rest(2)
    activate(3)
    wait_latents(3)
    each_tile(last_decode)

    @pl.when(outer)
    def _():
        place_rest(3)

    @pl.when(inner)
    def _():
        def far_tile(t):
            pass_on(1, t).wait_recv()
            add_to_part(2, t, from_far)
            pass_on(3, t).start()

        def last_hop(t):
            pass_on(4, t).wait_recv()
            add_to_part(1, t, across3)
            pass_on(0, t).start()

        def end_tile(t):
            place_tile(3, t)
            pass_on(2, t).wait_recv()
            add_to_part(3, t, from_end)
            pass_on(4, t).start()

            @pl.when(t >= 1)
            def _():
                last_hop(t - 1)

        each_tile(far_tile)
        each_tile(end_tile)
        last_hop(tiles - 1)

    def finish_tile(t):
        pass_on(0, t).wait_recv()
        cols = pl.ds(pl.multiple_of(t * TILE, TILE), TILE)
        diff = act[:, cols].astype(jnp.float32) - dec_bias[:, cols]
        diff = diff - part[0, t].astype(jnp.float32) - from_mate[t].astype(jnp.float32)
        return diff

    @pl.when(outer)
    def _():
        def tile(t):
            diff = finish_tile(t)
            acc[...] += diff * diff

        each_tile(tile)

    @pl.when(inner)
    def _():
        def tile(t):
            pass_on(3, t).wait_recv()
            diff = finish_tile(t) - across2[t].astype(jnp.float32)
            acc[...] += diff * diff

        each_tile(tile)

    stats[0:1] = jnp.sum(acc[...].T, axis=0, keepdims=True)
    stats[1:2] = jnp.sum(norm[...].T, axis=0, keepdims=True)
    stats[2:8] = jnp.zeros((6, tokens), jnp.float32)
    stat_copies = [
        remote(stats, stats_in.at[m], end_send.at[m], end_recv.at[m], tp_peer(m)) for m in range(1, 4)
    ]
    for copy in stat_copies:
        copy.start()
    for copy in stat_copies:
        copy.wait()
    both = (stats[...] + stats_in[1]) + (stats_in[2] + stats_in[3])
    error = both[0:1] / (both[1:2] + 1e-06)
    error_out[...] = jnp.broadcast_to(error, (8, tokens))
    mean_own[...] = jnp.broadcast_to(jnp.sum(error, axis=1, keepdims=True), (8, 128))
    mean_copies = [
        remote(mean_own, mean_in.at[m], end_send.at[3 + m], end_recv.at[3 + m], lat_peer(m))
        for m in range(1, 8)
    ]
    for copy in mean_copies:
        copy.start()
    for copy in mean_copies:
        copy.wait()
    low = (mean_own[...] + mean_in[1]) + (mean_in[2] + mean_in[3])
    high = (mean_in[4] + mean_in[5]) + (mean_in[6] + mean_in[7])
    mean_out[...] = (low + high) / (tokens * 8)

    for copy in meta_copies:
        copy.wait_send()
    each_tile(lambda t: hop(0, t).wait_send())
    for k in range(4):
        each_tile(lambda t: to_column(k, t).wait_send())
        for flow in (to_core, to_side, to_core2):
            each_half_tile(lambda t: flow(k, t).wait_send())
        each_tile(lambda t: back(k, t).wait_send())
    each_tile(lambda t: pass_on(0, t).wait_send())

    @pl.when(inner)
    def _():
        for flow in range(1, 5):
            each_tile(lambda t: hop(flow, t).wait_send())
        for flow in (3, 4):
            each_tile(lambda t: pass_on(flow, t).wait_send())

    @pl.when(outer)
    def _():
        for flow in (1, 2):
            each_tile(lambda t: pass_on(flow, t).wait_send())


def line_body(activations, active_blocks, enc_weight, enc_bias, dec_weight, dec_bias):
    tokens, active_count = active_blocks.shape
    capacity = 2 * tokens * active_count // 8
    width = activations.shape[1]
    block = enc_weight.shape[1]
    half = block // 2
    tiles = width // TILE
    names = jnp.pad(active_blocks.T, ((0, 8 - active_count), (0, 0)), constant_values=-1)
    bf, f32 = jnp.bfloat16, jnp.float32
    vm, dma = pltpu.VMEM, pltpu.SemaphoreType.DMA
    in_vmem = pl.BlockSpec(memory_space=pltpu.VMEM)
    anywhere = pl.BlockSpec(memory_space=pl.ANY)
    tiled = (tiles, tokens, TILE)
    error, mean = pl.pallas_call(
        functools.partial(line_kernel, tokens, capacity),
        out_shape=(jax.ShapeDtypeStruct((8, tokens), f32), jax.ShapeDtypeStruct((8, 128), f32)),
        in_specs=[in_vmem, in_vmem, anywhere, in_vmem, anywhere, in_vmem],
        out_specs=(in_vmem, in_vmem),
        scratch_shapes=[
            vm((width, block), bf), vm((block, width), bf),
            vm((4, tokens, width), bf), vm((4, 8, tokens), jnp.int32),
            vm((4, 2 * capacity, tokens), bf), vm((4, tokens, 2 * capacity), bf),
            vm((4, 2 * capacity, width), bf), vm((4, capacity, width), bf),
            vm((4, 2 * capacity, half), bf), vm((4, 2 * capacity, half), bf),
            vm((4, 2 * capacity, half), bf), vm((4, 2 * capacity, half), bf),
            vm((4, 2, 2 * capacity, half), bf),
            vm((4, tiles, capacity, TILE), bf), vm((4, tiles, 2 * capacity, TILE), bf),
            vm((4,) + tiled, bf),
            vm(tiled, bf), vm(tiled, bf), vm(tiled, bf), vm(tiled, bf), vm(tiled, bf),
            vm((tokens, TILE), f32), vm((tokens, TILE), f32),
            vm((8, tokens), f32), vm((4, 8, tokens), f32), vm((8, 128), f32), vm((8, 8, 128), f32),
            dma((2,)), dma((5, tiles)), dma((4, tiles)), dma((3,)), dma((4,)),
            dma((4, tiles)), dma((4, tiles)), dma((3, 4, half // TILE)), dma((3, 4, half // TILE)),
            dma((4, tiles)), dma((4, tiles)),
            dma((5, tiles)), dma((5, tiles)), dma((11,)), dma((11,)),
        ],
        compiler_params=pltpu.CompilerParams(
            collective_id=0, has_side_effects=True, vmem_limit_bytes=60 * 1024 * 1024
        ),
        cost_estimate=pl.CostEstimate(
            flops=4 * 8 * capacity * width * block, bytes_accessed=4 * width * block, transcendentals=0
        ),
    )(activations, names, enc_weight, enc_bias[None], dec_weight, dec_bias[None])
    return error[0], mean[0, 0]


def solution(mesh):
    in_specs = (P("lat", "tp"), P("lat", None), P("tp", "lat"), P("lat"), P("lat", "tp"), P("tp"))
    out_specs = (P("lat"), P())
    body = line_body if (mesh.shape["lat"], mesh.shape["tp"]) == (8, 4) else general_body
    return jax.shard_map(body, mesh=mesh, in_specs=in_specs, out_specs=out_specs, check_vma=False)
```

```python
import functools

import jax
import jax.numpy as jnp
from jax import lax
from jax.experimental import pallas as pl
from jax.experimental.pallas import tpu as pltpu
from jax.sharding import PartitionSpec as P


def score_slots(received, enc_weight, enc_bias, dec_weight):
    owners = received.shape[0]
    slot_count = received.shape[1]
    feature_part = received.shape[2]
    flat_rows = received.reshape(owners * slot_count, feature_part)
    partial_value = jnp.dot(flat_rows, enc_weight, preferred_element_type=jnp.float32)
    pre = lax.psum(partial_value.astype(jnp.bfloat16), "tp").astype(jnp.float32)
    latents = jnp.maximum(pre + enc_bias, 0.0).astype(jnp.bfloat16)
    decoded = jnp.dot(latents, dec_weight, preferred_element_type=jnp.float32).astype(jnp.bfloat16)
    decoded = decoded.reshape(owners, slot_count, feature_part)
    return lax.all_to_all(decoded, "lat", split_axis=0, concat_axis=0, tiled=True)


def finish(activations, summed, dec_bias, owners):
    token_count = activations.shape[0]
    recon = summed + dec_bias
    inputs_full = activations.astype(jnp.float32)
    diff = inputs_full - recon
    squares, norms = lax.psum(
        (jnp.sum(diff * diff, axis=1), jnp.sum(inputs_full * inputs_full, axis=1)), "tp"
    )
    token_error = squares / (norms + 1e-06)
    total = lax.psum(jnp.sum(token_error), "lat")
    mean_error = total / (token_count * owners)
    return (token_error, mean_error)


def general_body(activations, active_blocks, enc_weight, enc_bias, dec_weight, dec_bias):
    owners = lax.axis_size("lat")
    token_count, active_count = active_blocks.shape
    feature_part = activations.shape[1]
    capacity = 2 * token_count * active_count // owners
    centred = (activations.astype(jnp.float32) - dec_bias).astype(jnp.bfloat16)
    flat = active_blocks.reshape(-1)
    onehot = (flat[:, None] == jnp.arange(owners, dtype=jnp.int32)[None, :]).astype(jnp.int32)
    ranks = jnp.sum((jnp.cumsum(onehot, axis=0) - onehot) * onehot, axis=1)
    slot_rows = flat * capacity + ranks
    source_rows = jnp.repeat(centred, active_count, axis=0)
    outgoing = (
        jnp.zeros((owners * capacity, feature_part), jnp.bfloat16).at[slot_rows].set(source_rows)
    )
    outgoing = outgoing.reshape(owners, capacity, feature_part)
    received = lax.all_to_all(outgoing, "lat", split_axis=0, concat_axis=0, tiled=True)
    returned = score_slots(received, enc_weight, enc_bias, dec_weight)
    returned = returned.reshape(owners * capacity, feature_part)
    picked = returned[slot_rows].reshape(token_count, active_count, feature_part)
    return finish(activations, jnp.sum(picked.astype(jnp.float32), axis=1), dec_bias, owners)


MESH = pl.DeviceIdType.MESH
TILE = 256


def line_kernel(
    tokens, capacity,
    act, blocks, enc_hbm, enc_bias, dec_hbm, dec_bias,
    error_out, mean_out,
    enc, dec, src, meta, picks, places, rows, ysend, given, other, chip, side, lat,
    theirs, cat, part, from_mate, from_far, from_end, across2, across3,
    acc, norm, stats, stats_in, mean_own, mean_in,
    w_sem, hop_send, hop_recv, meta_send, meta_recv, col_send, col_recv, pair_send, pair_recv,
    back_send, back_recv, sum_send, sum_recv, end_send, end_recv,
):
    me, tp = lax.axis_index("lat"), lax.axis_index("tp")
    plane, column = me // 2, me % 2
    core = tp % 2
    inner = ((plane + 1) // 2) % 2 == 1
    outer = ((plane + 1) // 2) % 2 == 0
    width = act.shape[1]
    tiles = width // TILE
    half = enc.shape[1] // 2
    half_tiles = half // TILE

    def flip(value, mask):
        for bit in (1, 2, 4):
            if mask & bit:
                value = value + bit - 2 * bit * ((value // bit) % 2)
        return value

    def lat_peer(mask):
        return (flip(me, mask), tp)

    def tp_peer(mask):
        return (me, flip(tp, mask))

    MATE, ACROSS, OPPOSITE, COLUMN = 2, 6, 4, 1

    def columns(t, first=0):
        return pl.ds(pl.multiple_of(first + t * TILE, TILE), TILE)

    def remote(src_ref, dst_ref, send, recv, peer):
        return pltpu.make_async_remote_copy(
            src_ref=src_ref, dst_ref=dst_ref, send_sem=send, recv_sem=recv,
            device_id=peer, device_id_type=MESH,
        )

    enc_copy = pltpu.make_async_copy(enc_hbm, enc, w_sem.at[0])
    dec_copy = pltpu.make_async_copy(dec_hbm, dec, w_sem.at[1])
    enc_copy.start()
    dec_copy.start()

    def centre(t, carry):
        cols = pl.ds(pl.multiple_of(t * TILE, TILE), TILE)
        src[0, :, cols] = (act[:, cols].astype(jnp.float32) - dec_bias[cols][None]).astype(jnp.bfloat16)
        return carry

    lax.fori_loop(0, tiles, centre, 0)
    active_count = blocks.shape[0]
    meta[0, 0:active_count] = blocks[...]
    meta[0, active_count:8] = jnp.full((8 - active_count, tokens), -1, jnp.int32)

    barrier = pltpu.get_barrier_semaphore()
    for mask in range(1, 8):
        pl.semaphore_signal(barrier, inc=1, device_id=lat_peer(mask), device_id_type=MESH)
    for mask in range(1, 4):
        pl.semaphore_signal(barrier, inc=1, device_id=tp_peer(mask), device_id_type=MESH)
    pl.semaphore_wait(barrier, 10)

    far_slot = 3 - ((plane + 1) // 2) % 2
    meta_copies = [
        remote(meta.at[0], meta.at[1], meta_send.at[0], meta_recv.at[1], lat_peer(MATE)),
        remote(meta.at[0], meta.at[far_slot], meta_send.at[1], meta_recv.at[far_slot], lat_peer(ACROSS)),
        remote(meta.at[0], meta.at[far_slot], meta_send.at[2], meta_recv.at[far_slot], lat_peer(OPPOSITE)),
    ]
    for copy in meta_copies:
        copy.start()

    flows = [(0, 1, MATE), (0, 2, ACROSS), (2, 2, MATE), (1, 3, ACROSS), (3, 3, MATE)]

    def hop(flow, piece):
        here, there, mask = flows[flow]
        return remote(
            src.at[here, :, columns(piece)], src.at[there, :, columns(piece)],
            hop_send.at[flow, piece], hop_recv.at[there, piece], lat_peer(mask),
        )

    def each_tile(fn, first=0, last=tiles):
        lax.fori_loop(first, last, lambda t, carry: (fn(t), carry)[1], 0)

    def each_half_tile(fn):
        lax.fori_loop(0, half_tiles, lambda t, carry: (fn(t), carry)[1], 0)

    def first_hops(t):
        hop(0, t).start()

        @pl.when(inner)
        def _():
            hop(1, t).start()

    each_tile(first_hops)

    def squares_of_inputs(t):
        cols = pl.ds(pl.multiple_of(t * TILE, TILE), TILE)
        value = act[:, cols].astype(jnp.float32)
        norm[...] += value * value

    norm[...] = jnp.zeros_like(norm)
    acc[...] = jnp.zeros_like(acc)
    each_tile(squares_of_inputs)

    earlier = (
        lax.broadcasted_iota(jnp.int32, (tokens, tokens), 0)
        < lax.broadcasted_iota(jnp.int32, (tokens, tokens), 1)
    ).astype(jnp.float32).astype(jnp.bfloat16)
    slots = lax.broadcasted_iota(jnp.int32, (capacity, tokens), 0).astype(jnp.float32)

    def make_picks(k):
        names = meta[k]
        named = []
        for owner in (me, flip(me, COLUMN)):
            hit = jnp.max((names == owner).astype(jnp.float32), axis=0, keepdims=True)
            named.append(jnp.broadcast_to(hit, (8, tokens)))
        named = jnp.concatenate(named)
        ranks = jnp.dot(named.astype(jnp.bfloat16), earlier, preferred_element_type=jnp.float32)
        pick = jnp.concatenate([
            jnp.where(ranks[8 * i:8 * i + 1] == slots, named[8 * i:8 * i + 1], 0.0)
            for i in range(2)
        ])
        picks[k] = pick.astype(jnp.bfloat16)
        places[k] = pick.T.astype(jnp.bfloat16)

    def to_column(k, t):
        return remote(
            ysend.at[k, :, columns(t)], rows.at[k, pl.ds(capacity, capacity), columns(t)],
            col_send.at[k, t], col_recv.at[k, t], lat_peer(COLUMN),
        )

    def to_core(k, t):
        return remote(
            given.at[k, :, columns(t)], other.at[k, :, columns(t)],
            pair_send.at[0, k, t], pair_recv.at[0, k, t], tp_peer(1),
        )

    def to_side(k, t):
        return remote(
            chip.at[k, :, columns(t)], side.at[k, :, columns(t)],
            pair_send.at[1, k, t], pair_recv.at[1, k, t], tp_peer(2),
        )

    def to_core2(k, t):
        return remote(
            lat.at[k, core, :, columns(t)], lat.at[k, core, :, columns(t)],
            pair_send.at[2, k, t], pair_recv.at[2, k, t], tp_peer(1),
        )

    def pick_tile(k, t):
        got = jnp.dot(picks[k], src[k, :, columns(t)], preferred_element_type=jnp.float32)
        got = got.astype(jnp.bfloat16)
        rows[k, pl.ds(0, capacity), columns(t)] = got[:capacity]
        ysend[k, :, columns(t)] = got[capacity:]
        to_column(k, t).start()

    def encode(k):
        each_tile(lambda t: to_column(k, t).wait_recv())

        def give(t):
            cols = columns(t, (1 - core) * half)
            value = jnp.dot(rows[k], enc[:, cols], preferred_element_type=jnp.float32)
            given[k, :, columns(t)] = value.astype(jnp.bfloat16)
            to_core(k, t).start()

        def keep(t):
            cols = columns(t, core * half)
            value = jnp.dot(rows[k], enc[:, cols], preferred_element_type=jnp.float32)
            to_core(k, t).wait_recv()
            value += other[k, :, columns(t)].astype(jnp.float32)
            chip[k, :, columns(t)] = value.astype(jnp.bfloat16)
            to_side(k, t).start()

        each_half_tile(give)
        each_half_tile(keep)

    def activate(k):
        def tile(t):
            to_side(k, t).wait_recv()
            bias = enc_bias[columns(t, core * half)][None]
            pre = chip[k, :, columns(t)].astype(jnp.float32) + side[k, :, columns(t)].astype(jnp.float32)
            lat[k, core, :, columns(t)] = jnp.maximum(pre + bias, 0.0).astype(jnp.bfloat16)
            to_core2(k, t).start()

        each_half_tile(tile)

    def back(k, t):
        return remote(
            theirs.at[k, t], cat.at[k, t, pl.ds(capacity, capacity)],
            back_send.at[k, t], back_recv.at[k, t], lat_peer(COLUMN),
        )

    def wait_latents(k):
        each_half_tile(lambda t: to_core2(k, t).wait_recv())

    def decode_tile(k, t):
        cols = columns(t)
        value = jnp.dot(lat[k, 0], dec[pl.ds(0, half), cols], preferred_element_type=jnp.float32)
        value += jnp.dot(lat[k, 1], dec[pl.ds(half, half), cols], preferred_element_type=jnp.float32)
        value = value.astype(jnp.bfloat16)
        cat[k, t, pl.ds(0, capacity)] = value[:capacity]
        theirs[k, t] = value[capacity:]
        if k >= 1:
            back(k, t).start()

    sums = [(1, from_mate, MATE), (2, from_far, MATE), (3, from_end, MATE), (2, across2, ACROSS), (3, across3, ACROSS)]

    def pass_on(flow, t):
        k, target, mask = sums[flow]
        return remote(
            part.at[k, t], target.at[t], sum_send.at[flow, t], sum_recv.at[flow, t], lat_peer(mask)
        )

    def add_to_part(k, t, more):
        part[k, t] = (part[k, t].astype(jnp.float32) + more[t].astype(jnp.float32)).astype(jnp.bfloat16)

    def place_tile(k, t):
        back(k, t).wait_recv()
        value = jnp.dot(places[k], cat[k, t], preferred_element_type=jnp.float32)
        part[k, t] = value.astype(jnp.bfloat16)
        if k >= 1:
            @pl.when(outer)
            def _():
                pass_on(k - 1, t).start()

    LAG = 3

    def place_behind(k, t):
        @pl.when(t >= LAG)
        def _():
            place_tile(k, t - LAG)

    def place_rest(k):
        each_tile(lambda t: place_tile(k, t), tiles - LAG)

    meta_done = [
        remote(meta.at[0], meta.at[k], meta_send.at[0], meta_recv.at[k], lat_peer(MATE))
        for k in range(1, 4)
    ]

    make_picks(0)
    each_tile(lambda t: pick_tile(0, t))
    for k in range(1, 4):
        meta_done[k - 1].wait_recv()
        make_picks(k)

    def mate_arrives(t):
        @pl.when(inner)
        def _():
            hop(1, t).wait_recv()
            hop(2, t).start()

        hop(0, t).wait_recv()

        @pl.when(inner)
        def _():
            hop(3, t).start()

        pick_tile(1, t)

    def far_inner_arrives(t):
        @pl.when(outer)
        def _():
            hop(2, t).wait_recv()

        @pl.when(inner)
        def _():
            hop(3, t).wait_recv()
            hop(4, t).start()

        pick_tile(2, t)
        decode_tile(0, t)

    def far_outer_arrives(t):
        @pl.when(outer)
        def _():
            hop(3, t).wait_recv()

        pick_tile(3, t)
        place_tile(1, t)

    def third_decode(t):
        decode_tile(2, t)
        place_behind(2, t)

    def last_decode(t):
        decode_tile(3, t)

        @pl.when(outer)
        def _():
            place_behind(3, t)

    each_tile(mate_arrives, 0, tiles // 2)
    enc_copy.wait()
    encode(0)
    each_tile(mate_arrives, tiles // 2, tiles)
    encode(1)
    activate(0)
    dec_copy.wait()
    wait_latents(0)
    each_tile(far_inner_arrives, 0, tiles - 2)
    activate(1)
    each_tile(far_inner_arrives, tiles - 2, tiles)
    wait_latents(1)
    each_tile(lambda t: decode_tile(1, t))
    encode(2)
    each_tile(far_outer_arrives)
    activate(2)
    encode(3)
    wait_latents(2)
    each_tile(third_decode)
    place_rest(2)
    activate(3)
    wait_latents(3)
    each_tile(last_decode)
    each_tile(lambda t: back(0, t).start())

    @pl.when(outer)
    def _():
        place_rest(3)
        each_tile(lambda t: place_tile(0, t))

    @pl.when(inner)
    def _():
        def far_tile(t):
            pass_on(1, t).wait_recv()
            add_to_part(2, t, from_far)
            pass_on(3, t).start()
            place_tile(0, t)

        def last_hop(t):
            pass_on(4, t).wait_recv()
            add_to_part(1, t, across3)
            pass_on(0, t).start()

        def end_tile(t):
            place_tile(3, t)
            pass_on(2, t).wait_recv()
            add_to_part(3, t, from_end)
            pass_on(4, t).start()

            @pl.when(t >= 1)
            def _():
                last_hop(t - 1)

        each_tile(far_tile)
        each_tile(end_tile)
        last_hop(tiles - 1)

    def finish_tile(t):
        pass_on(0, t).wait_recv()
        cols = pl.ds(pl.multiple_of(t * TILE, TILE), TILE)
        diff = act[:, cols].astype(jnp.float32) - dec_bias[cols][None]
        diff = diff - part[0, t].astype(jnp.float32) - from_mate[t].astype(jnp.float32)
        return diff

    @pl.when(outer)
    def _():
        def tile(t):
            diff = finish_tile(t)
            acc[...] += diff * diff

        each_tile(tile)

    @pl.when(inner)
    def _():
        def tile(t):
            pass_on(3, t).wait_recv()
            diff = finish_tile(t) - across2[t].astype(jnp.float32)
            acc[...] += diff * diff

        each_tile(tile)

    stats[0:1] = jnp.sum(acc[...].T, axis=0, keepdims=True)
    stats[1:2] = jnp.sum(norm[...].T, axis=0, keepdims=True)
    stats[2:8] = jnp.zeros((6, tokens), jnp.float32)
    stat_copies = [
        remote(stats, stats_in.at[m], end_send.at[m], end_recv.at[m], tp_peer(m)) for m in range(1, 4)
    ]
    for copy in stat_copies:
        copy.start()
    for copy in stat_copies:
        copy.wait()
    both = (stats[...] + stats_in[1]) + (stats_in[2] + stats_in[3])
    error = both[0:1] / (both[1:2] + 1e-06)
    error_out[...] = error[0]
    mean_own[...] = jnp.broadcast_to(jnp.sum(error, axis=1, keepdims=True), (8, 128))
    mean_copies = [
        remote(mean_own, mean_in.at[m], end_send.at[3 + m], end_recv.at[3 + m], lat_peer(m))
        for m in range(1, 8)
    ]
    for copy in mean_copies:
        copy.start()
    for copy in mean_copies:
        copy.wait()
    low = (mean_own[...] + mean_in[1]) + (mean_in[2] + mean_in[3])
    high = (mean_in[4] + mean_in[5]) + (mean_in[6] + mean_in[7])
    mean_out[0, 0] = jnp.max((low + high) / (tokens * 8))

    for copy in meta_copies:
        copy.wait_send()
    each_tile(lambda t: hop(0, t).wait_send())
    for k in range(4):
        each_tile(lambda t: to_column(k, t).wait_send())
        for flow in (to_core, to_side, to_core2):
            each_half_tile(lambda t: flow(k, t).wait_send())
        each_tile(lambda t: back(k, t).wait_send())
    each_tile(lambda t: pass_on(0, t).wait_send())

    @pl.when(inner)
    def _():
        for flow in range(1, 5):
            each_tile(lambda t: hop(flow, t).wait_send())
        for flow in (3, 4):
            each_tile(lambda t: pass_on(flow, t).wait_send())

    @pl.when(outer)
    def _():
        for flow in (1, 2):
            each_tile(lambda t: pass_on(flow, t).wait_send())


def line_body(activations, active_blocks, enc_weight, enc_bias, dec_weight, dec_bias):
    tokens, active_count = active_blocks.shape
    capacity = 2 * tokens * active_count // 8
    width = activations.shape[1]
    block = enc_weight.shape[1]
    half = block // 2
    tiles = width // TILE
    bf, f32 = jnp.bfloat16, jnp.float32
    vm, dma = pltpu.VMEM, pltpu.SemaphoreType.DMA
    in_vmem = pl.BlockSpec(memory_space=pltpu.VMEM)
    anywhere = pl.BlockSpec(memory_space=pl.ANY)
    tiled = (tiles, tokens, TILE)
    error, mean = pl.pallas_call(
        functools.partial(line_kernel, tokens, capacity),
        out_shape=(jax.ShapeDtypeStruct((tokens,), f32), jax.ShapeDtypeStruct((1, 1), f32)),
        in_specs=[in_vmem, in_vmem, anywhere, in_vmem, anywhere, in_vmem],
        out_specs=(in_vmem, pl.BlockSpec(memory_space=pltpu.SMEM)),
        scratch_shapes=[
            vm((width, block), bf), vm((block, width), bf),
            vm((4, tokens, width), bf), vm((4, 8, tokens), jnp.int32),
            vm((4, 2 * capacity, tokens), bf), vm((4, tokens, 2 * capacity), bf),
            vm((4, 2 * capacity, width), bf), vm((4, capacity, width), bf),
            vm((4, 2 * capacity, half), bf), vm((4, 2 * capacity, half), bf),
            vm((4, 2 * capacity, half), bf), vm((4, 2 * capacity, half), bf),
            vm((4, 2, 2 * capacity, half), bf),
            vm((4, tiles, capacity, TILE), bf), vm((4, tiles, 2 * capacity, TILE), bf),
            vm((4,) + tiled, bf),
            vm(tiled, bf), vm(tiled, bf), vm(tiled, bf), vm(tiled, bf), vm(tiled, bf),
            vm((tokens, TILE), f32), vm((tokens, TILE), f32),
            vm((8, tokens), f32), vm((4, 8, tokens), f32), vm((8, 128), f32), vm((8, 8, 128), f32),
            dma((2,)), dma((5, tiles)), dma((4, tiles)), dma((3,)), dma((4,)),
            dma((4, tiles)), dma((4, tiles)), dma((3, 4, half // TILE)), dma((3, 4, half // TILE)),
            dma((4, tiles)), dma((4, tiles)),
            dma((5, tiles)), dma((5, tiles)), dma((11,)), dma((11,)),
        ],
        compiler_params=pltpu.CompilerParams(
            collective_id=0, has_side_effects=True, vmem_limit_bytes=60 * 1024 * 1024
        ),
        cost_estimate=pl.CostEstimate(
            flops=4 * 8 * capacity * width * block, bytes_accessed=4 * width * block, transcendentals=0
        ),
    )(activations, active_blocks.T, enc_weight, enc_bias, dec_weight, dec_bias)
    return error, mean[0, 0]


def solution(mesh):
    in_specs = (P("lat", "tp"), P("lat", None), P("tp", "lat"), P("lat"), P("lat", "tp"), P("tp"))
    out_specs = (P("lat"), P())
    body = line_body if (mesh.shape["lat"], mesh.shape["tp"]) == (8, 4) else general_body
    return jax.shard_map(body, mesh=mesh, in_specs=in_specs, out_specs=out_specs, check_vma=False)
```

```python
import functools

import jax
import jax.numpy as jnp
from jax import lax
from jax.experimental import pallas as pl
from jax.experimental.pallas import tpu as pltpu
from jax.sharding import PartitionSpec as P


def score_slots(received, enc_weight, enc_bias, dec_weight):
    owners = received.shape[0]
    slot_count = received.shape[1]
    feature_part = received.shape[2]
    flat_rows = received.reshape(owners * slot_count, feature_part)
    partial_value = jnp.dot(flat_rows, enc_weight, preferred_element_type=jnp.float32)
    pre = lax.psum(partial_value.astype(jnp.bfloat16), "tp").astype(jnp.float32)
    latents = jnp.maximum(pre + enc_bias, 0.0).astype(jnp.bfloat16)
    decoded = jnp.dot(latents, dec_weight, preferred_element_type=jnp.float32).astype(jnp.bfloat16)
    decoded = decoded.reshape(owners, slot_count, feature_part)
    return lax.all_to_all(decoded, "lat", split_axis=0, concat_axis=0, tiled=True)


def finish(activations, summed, dec_bias, owners):
    token_count = activations.shape[0]
    recon = summed + dec_bias
    inputs_full = activations.astype(jnp.float32)
    diff = inputs_full - recon
    squares, norms = lax.psum(
        (jnp.sum(diff * diff, axis=1), jnp.sum(inputs_full * inputs_full, axis=1)), "tp"
    )
    token_error = squares / (norms + 1e-06)
    total = lax.psum(jnp.sum(token_error), "lat")
    mean_error = total / (token_count * owners)
    return (token_error, mean_error)


def general_body(activations, active_blocks, enc_weight, enc_bias, dec_weight, dec_bias):
    owners = lax.axis_size("lat")
    token_count, active_count = active_blocks.shape
    feature_part = activations.shape[1]
    capacity = 2 * token_count * active_count // owners
    centred = (activations.astype(jnp.float32) - dec_bias).astype(jnp.bfloat16)
    flat = active_blocks.reshape(-1)
    onehot = (flat[:, None] == jnp.arange(owners, dtype=jnp.int32)[None, :]).astype(jnp.int32)
    ranks = jnp.sum((jnp.cumsum(onehot, axis=0) - onehot) * onehot, axis=1)
    slot_rows = flat * capacity + ranks
    source_rows = jnp.repeat(centred, active_count, axis=0)
    outgoing = (
        jnp.zeros((owners * capacity, feature_part), jnp.bfloat16).at[slot_rows].set(source_rows)
    )
    outgoing = outgoing.reshape(owners, capacity, feature_part)
    received = lax.all_to_all(outgoing, "lat", split_axis=0, concat_axis=0, tiled=True)
    returned = score_slots(received, enc_weight, enc_bias, dec_weight)
    returned = returned.reshape(owners * capacity, feature_part)
    picked = returned[slot_rows].reshape(token_count, active_count, feature_part)
    return finish(activations, jnp.sum(picked.astype(jnp.float32), axis=1), dec_bias, owners)


MESH = pl.DeviceIdType.MESH
TILE = 256


def line_kernel(
    tokens, capacity,
    act, blocks, enc_hbm, enc_bias, dec_hbm, dec_bias,
    error_out, mean_out,
    enc, dec, src, meta, picks, places, rows, ysend, given, other, chip, side, lat,
    theirs, cat, part, from_mate, from_far, from_end, across2, across3,
    acc, norm, stats, stats_in, mean_own, mean_in,
    w_sem, hop_send, hop_recv, meta_send, meta_recv, col_send, col_recv, pair_send, pair_recv,
    back_send, back_recv, sum_send, sum_recv, end_send, end_recv,
):
    me, tp = lax.axis_index("lat"), lax.axis_index("tp")
    plane, column = me // 2, me % 2
    core = tp % 2
    inner = ((plane + 1) // 2) % 2 == 1
    outer = ((plane + 1) // 2) % 2 == 0
    width = act.shape[1]
    tiles = width // TILE
    half = enc.shape[1] // 2
    half_tiles = half // TILE

    def flip(value, mask):
        for bit in (1, 2, 4):
            if mask & bit:
                value = value + bit - 2 * bit * ((value // bit) % 2)
        return value

    def lat_peer(mask):
        return (flip(me, mask), tp)

    def tp_peer(mask):
        return (me, flip(tp, mask))

    MATE, ACROSS, OPPOSITE, COLUMN = 2, 6, 4, 1

    def columns(t, first=0):
        return pl.ds(pl.multiple_of(first + t * TILE, TILE), TILE)

    def remote(src_ref, dst_ref, send, recv, peer):
        return pltpu.make_async_remote_copy(
            src_ref=src_ref, dst_ref=dst_ref, send_sem=send, recv_sem=recv,
            device_id=peer, device_id_type=MESH,
        )

    enc_copy = pltpu.make_async_copy(enc_hbm, enc, w_sem.at[0])
    dec_copy = pltpu.make_async_copy(dec_hbm, dec, w_sem.at[1])
    enc_copy.start()
    dec_copy.start()

    def centre(t, carry):
        cols = pl.ds(pl.multiple_of(t * TILE, TILE), TILE)
        src[0, :, cols] = (act[:, cols].astype(jnp.float32) - dec_bias[cols][None]).astype(jnp.bfloat16)
        return carry

    lax.fori_loop(0, tiles, centre, 0)
    active_count = blocks.shape[0]
    meta[0, 0:active_count] = blocks[...]
    meta[0, active_count:8] = jnp.full((8 - active_count, tokens), -1, jnp.int32)

    barrier = pltpu.get_barrier_semaphore()
    for mask in range(1, 8):
        pl.semaphore_signal(barrier, inc=1, device_id=lat_peer(mask), device_id_type=MESH)
    for mask in range(1, 4):
        pl.semaphore_signal(barrier, inc=1, device_id=tp_peer(mask), device_id_type=MESH)
    pl.semaphore_wait(barrier, 10)

    far_slot = 3 - ((plane + 1) // 2) % 2
    meta_copies = [
        remote(meta.at[0], meta.at[1], meta_send.at[0], meta_recv.at[1], lat_peer(MATE)),
        remote(meta.at[0], meta.at[far_slot], meta_send.at[1], meta_recv.at[far_slot], lat_peer(ACROSS)),
        remote(meta.at[0], meta.at[far_slot], meta_send.at[2], meta_recv.at[far_slot], lat_peer(OPPOSITE)),
    ]
    for copy in meta_copies:
        copy.start()

    flows = [(0, 1, MATE), (0, 2, ACROSS), (2, 2, MATE), (1, 3, ACROSS), (3, 3, MATE)]

    def hop(flow, piece):
        here, there, mask = flows[flow]
        return remote(
            src.at[here, :, columns(piece)], src.at[there, :, columns(piece)],
            hop_send.at[flow, piece], hop_recv.at[there, piece], lat_peer(mask),
        )

    def each_tile(fn, first=0, last=tiles):
        lax.fori_loop(first, last, lambda t, carry: (fn(t), carry)[1], 0)

    def each_half_tile(fn):
        lax.fori_loop(0, half_tiles, lambda t, carry: (fn(t), carry)[1], 0)

    def first_hops(t):
        hop(0, t).start()

        @pl.when(inner)
        def _():
            hop(1, t).start()

    each_tile(first_hops)

    def squares_of_inputs(t):
        cols = pl.ds(pl.multiple_of(t * TILE, TILE), TILE)
        value = act[:, cols].astype(jnp.float32)
        norm[...] += value * value

    norm[...] = jnp.zeros_like(norm)
    acc[...] = jnp.zeros_like(acc)
    each_tile(squares_of_inputs)

    earlier = (
        lax.broadcasted_iota(jnp.int32, (tokens, tokens), 0)
        < lax.broadcasted_iota(jnp.int32, (tokens, tokens), 1)
    ).astype(jnp.float32).astype(jnp.bfloat16)
    slots = lax.broadcasted_iota(jnp.int32, (capacity, tokens), 0).astype(jnp.float32)

    def make_picks(k):
        names = meta[k]
        named = []
        for owner in (me, flip(me, COLUMN)):
            hit = jnp.max((names == owner).astype(jnp.float32), axis=0, keepdims=True)
            named.append(jnp.broadcast_to(hit, (8, tokens)))
        named = jnp.concatenate(named)
        ranks = jnp.dot(named.astype(jnp.bfloat16), earlier, preferred_element_type=jnp.float32)
        pick = jnp.concatenate([
            jnp.where(ranks[8 * i:8 * i + 1] == slots, named[8 * i:8 * i + 1], 0.0)
            for i in range(2)
        ])
        picks[k] = pick.astype(jnp.bfloat16)
        places[k] = pick.T.astype(jnp.bfloat16)

    def to_column(k, t):
        return remote(
            ysend.at[k, :, columns(t)], rows.at[k, pl.ds(capacity, capacity), columns(t)],
            col_send.at[k, t], col_recv.at[k, t], lat_peer(COLUMN),
        )

    def to_core(k, t):
        return remote(
            given.at[k, :, columns(t)], other.at[k, :, columns(t)],
            pair_send.at[0, k, t], pair_recv.at[0, k, t], tp_peer(1),
        )

    def to_side(k, t):
        return remote(
            chip.at[k, :, columns(t)], side.at[k, :, columns(t)],
            pair_send.at[1, k, t], pair_recv.at[1, k, t], tp_peer(2),
        )

    def to_core2(k, t):
        return remote(
            lat.at[k, core, :, columns(t)], lat.at[k, core, :, columns(t)],
            pair_send.at[2, k, t], pair_recv.at[2, k, t], tp_peer(1),
        )

    def pick_tile(k, t):
        got = jnp.dot(picks[k], src[k, :, columns(t)], preferred_element_type=jnp.float32)
        got = got.astype(jnp.bfloat16)
        rows[k, pl.ds(0, capacity), columns(t)] = got[:capacity]
        ysend[k, :, columns(t)] = got[capacity:]
        to_column(k, t).start()

    def encode(k):
        each_tile(lambda t: to_column(k, t).wait_recv())

        def give(t):
            cols = columns(t, (1 - core) * half)
            value = jnp.dot(rows[k], enc[:, cols], preferred_element_type=jnp.float32)
            given[k, :, columns(t)] = value.astype(jnp.bfloat16)
            to_core(k, t).start()

        def keep(t):
            cols = columns(t, core * half)
            value = jnp.dot(rows[k], enc[:, cols], preferred_element_type=jnp.float32)
            to_core(k, t).wait_recv()
            value += other[k, :, columns(t)].astype(jnp.float32)
            chip[k, :, columns(t)] = value.astype(jnp.bfloat16)
            to_side(k, t).start()

        each_half_tile(give)
        each_half_tile(keep)

    def activate(k):
        def tile(t):
            to_side(k, t).wait_recv()
            bias = enc_bias[columns(t, core * half)][None]
            pre = chip[k, :, columns(t)].astype(jnp.float32) + side[k, :, columns(t)].astype(jnp.float32)
            lat[k, core, :, columns(t)] = jnp.maximum(pre + bias, 0.0).astype(jnp.bfloat16)
            to_core2(k, t).start()

        each_half_tile(tile)

    def back(k, t):
        return remote(
            theirs.at[k, t], cat.at[k, t, pl.ds(capacity, capacity)],
            back_send.at[k, t], back_recv.at[k, t], lat_peer(COLUMN),
        )

    def wait_latents(k):
        each_half_tile(lambda t: to_core2(k, t).wait_recv())

    def decode_tile(k, t):
        cols = columns(t)
        value = jnp.dot(lat[k, 0], dec[pl.ds(0, half), cols], preferred_element_type=jnp.float32)
        value += jnp.dot(lat[k, 1], dec[pl.ds(half, half), cols], preferred_element_type=jnp.float32)
        value = value.astype(jnp.bfloat16)
        cat[k, t, pl.ds(0, capacity)] = value[:capacity]
        theirs[k, t] = value[capacity:]
        if k >= 1:
            back(k, t).start()

    sums = [(1, from_mate, MATE), (2, from_far, MATE), (3, from_end, MATE), (2, across2, ACROSS), (3, across3, ACROSS)]

    def pass_on(flow, t):
        k, target, mask = sums[flow]
        return remote(
            part.at[k, t], target.at[t], sum_send.at[flow, t], sum_recv.at[flow, t], lat_peer(mask)
        )

    def add_to_part(k, t, more):
        part[k, t] = (part[k, t].astype(jnp.float32) + more[t].astype(jnp.float32)).astype(jnp.bfloat16)

    def place_tile(k, t):
        back(k, t).wait_recv()
        value = jnp.dot(places[k], cat[k, t], preferred_element_type=jnp.float32)
        part[k, t] = value.astype(jnp.bfloat16)
        if k >= 1:
            @pl.when(outer)
            def _():
                pass_on(k - 1, t).start()

    LAG = 3

    def place_behind(k, t):
        @pl.when(t >= LAG)
        def _():
            place_tile(k, t - LAG)

    def place_rest(k):
        each_tile(lambda t: place_tile(k, t), tiles - LAG)

    meta_done = [
        remote(meta.at[0], meta.at[k], meta_send.at[0], meta_recv.at[k], lat_peer(MATE))
        for k in range(1, 4)
    ]

    make_picks(0)
    each_tile(lambda t: pick_tile(0, t))
    for k in range(1, 4):
        meta_done[k - 1].wait_recv()
        make_picks(k)

    def mate_arrives(t):
        @pl.when(inner)
        def _():
            hop(1, t).wait_recv()
            hop(2, t).start()

        hop(0, t).wait_recv()

        @pl.when(inner)
        def _():
            hop(3, t).start()

        pick_tile(1, t)

    def far_inner_arrives(t):
        @pl.when(outer)
        def _():
            hop(2, t).wait_recv()

        @pl.when(inner)
        def _():
            hop(3, t).wait_recv()
            hop(4, t).start()

        pick_tile(2, t)

        @pl.when(inner)
        def _():
            decode_tile(0, t)

    def far_outer_arrives(t):
        @pl.when(outer)
        def _():
            hop(3, t).wait_recv()

        pick_tile(3, t)

    def second_decode(t):
        decode_tile(1, t)
        place_behind(1, t)

    def third_decode(t):
        decode_tile(2, t)
        place_behind(2, t)

    def last_decode(t):
        decode_tile(3, t)

        @pl.when(outer)
        def _():
            place_behind(3, t)

    each_tile(mate_arrives, 0, tiles // 2)
    enc_copy.wait()
    encode(0)
    each_tile(mate_arrives, tiles // 2, tiles)
    encode(1)
    activate(0)
    dec_copy.wait()
    wait_latents(0)
    each_tile(far_inner_arrives)
    activate(1)
    wait_latents(1)
    each_tile(second_decode)
    encode(2)
    place_rest(1)
    each_tile(far_outer_arrives)
    activate(2)
    encode(3)
    wait_latents(2)
    each_tile(third_decode)
    place_rest(2)
    activate(3)
    wait_latents(3)
    each_tile(last_decode)

    @pl.when(outer)
    def _():
        def own_decode(t):
            decode_tile(0, t)
            back(0, t).start()

        place_rest(3)
        each_tile(own_decode)
        each_tile(lambda t: place_tile(0, t))

    @pl.when(inner)
    def _():
        def far_tile(t):
            pass_on(1, t).wait_recv()
            add_to_part(2, t, from_far)
            pass_on(3, t).start()
            place_tile(0, t)

        def last_hop(t):
            pass_on(4, t).wait_recv()
            add_to_part(1, t, across3)
            pass_on(0, t).start()

        def end_tile(t):
            place_tile(3, t)
            pass_on(2, t).wait_recv()
            add_to_part(3, t, from_end)
            pass_on(4, t).start()

            @pl.when(t >= 1)
            def _():
                last_hop(t - 1)

        each_tile(lambda t: back(0, t).start())
        each_tile(far_tile)
        each_tile(end_tile)
        last_hop(tiles - 1)

    def finish_tile(t):
        pass_on(0, t).wait_recv()
        cols = pl.ds(pl.multiple_of(t * TILE, TILE), TILE)
        diff = act[:, cols].astype(jnp.float32) - dec_bias[cols][None]
        diff = diff - part[0, t].astype(jnp.float32) - from_mate[t].astype(jnp.float32)
        return diff

    @pl.when(outer)
    def _():
        def tile(t):
            diff = finish_tile(t)
            acc[...] += diff * diff

        each_tile(tile)

    @pl.when(inner)
    def _():
        def tile(t):
            pass_on(3, t).wait_recv()
            diff = finish_tile(t) - across2[t].astype(jnp.float32)
            acc[...] += diff * diff

        each_tile(tile)

    stats[0:1] = jnp.sum(acc[...].T, axis=0, keepdims=True)
    stats[1:2] = jnp.sum(norm[...].T, axis=0, keepdims=True)
    stats[2:8] = jnp.zeros((6, tokens), jnp.float32)
    stat_copies = [
        remote(stats, stats_in.at[m], end_send.at[m], end_recv.at[m], tp_peer(m)) for m in range(1, 4)
    ]
    for copy in stat_copies:
        copy.start()
    for copy in stat_copies:
        copy.wait()
    both = (stats[...] + stats_in[1]) + (stats_in[2] + stats_in[3])
    error = both[0:1] / (both[1:2] + 1e-06)
    error_out[...] = error[0]
    mean_own[...] = jnp.broadcast_to(jnp.sum(error, axis=1, keepdims=True), (8, 128))
    mean_copies = [
        remote(mean_own, mean_in.at[m], end_send.at[3 + m], end_recv.at[3 + m], lat_peer(m))
        for m in range(1, 8)
    ]
    for copy in mean_copies:
        copy.start()
    for copy in mean_copies:
        copy.wait()
    low = (mean_own[...] + mean_in[1]) + (mean_in[2] + mean_in[3])
    high = (mean_in[4] + mean_in[5]) + (mean_in[6] + mean_in[7])
    mean_out[0, 0] = jnp.max((low + high) / (tokens * 8))

    for copy in meta_copies:
        copy.wait_send()
    each_tile(lambda t: hop(0, t).wait_send())
    for k in range(4):
        each_tile(lambda t: to_column(k, t).wait_send())
        for flow in (to_core, to_side, to_core2):
            each_half_tile(lambda t: flow(k, t).wait_send())
        each_tile(lambda t: back(k, t).wait_send())
    each_tile(lambda t: pass_on(0, t).wait_send())

    @pl.when(inner)
    def _():
        for flow in range(1, 5):
            each_tile(lambda t: hop(flow, t).wait_send())
        for flow in (3, 4):
            each_tile(lambda t: pass_on(flow, t).wait_send())

    @pl.when(outer)
    def _():
        for flow in (1, 2):
            each_tile(lambda t: pass_on(flow, t).wait_send())


def line_body(activations, active_blocks, enc_weight, enc_bias, dec_weight, dec_bias):
    tokens, active_count = active_blocks.shape
    capacity = 2 * tokens * active_count // 8
    width = activations.shape[1]
    block = enc_weight.shape[1]
    half = block // 2
    tiles = width // TILE
    bf, f32 = jnp.bfloat16, jnp.float32
    vm, dma = pltpu.VMEM, pltpu.SemaphoreType.DMA
    in_vmem = pl.BlockSpec(memory_space=pltpu.VMEM)
    anywhere = pl.BlockSpec(memory_space=pl.ANY)
    tiled = (tiles, tokens, TILE)
    error, mean = pl.pallas_call(
        functools.partial(line_kernel, tokens, capacity),
        out_shape=(jax.ShapeDtypeStruct((tokens,), f32), jax.ShapeDtypeStruct((1, 1), f32)),
        in_specs=[in_vmem, in_vmem, anywhere, in_vmem, anywhere, in_vmem],
        out_specs=(in_vmem, pl.BlockSpec(memory_space=pltpu.SMEM)),
        scratch_shapes=[
            vm((width, block), bf), vm((block, width), bf),
            vm((4, tokens, width), bf), vm((4, 8, tokens), jnp.int32),
            vm((4, 2 * capacity, tokens), bf), vm((4, tokens, 2 * capacity), bf),
            vm((4, 2 * capacity, width), bf), vm((4, capacity, width), bf),
            vm((4, 2 * capacity, half), bf), vm((4, 2 * capacity, half), bf),
            vm((4, 2 * capacity, half), bf), vm((4, 2 * capacity, half), bf),
            vm((4, 2, 2 * capacity, half), bf),
            vm((4, tiles, capacity, TILE), bf), vm((4, tiles, 2 * capacity, TILE), bf),
            vm((4,) + tiled, bf),
            vm(tiled, bf), vm(tiled, bf), vm(tiled, bf), vm(tiled, bf), vm(tiled, bf),
            vm((tokens, TILE), f32), vm((tokens, TILE), f32),
            vm((8, tokens), f32), vm((4, 8, tokens), f32), vm((8, 128), f32), vm((8, 8, 128), f32),
            dma((2,)), dma((5, tiles)), dma((4, tiles)), dma((3,)), dma((4,)),
            dma((4, tiles)), dma((4, tiles)), dma((3, 4, half // TILE)), dma((3, 4, half // TILE)),
            dma((4, tiles)), dma((4, tiles)),
            dma((5, tiles)), dma((5, tiles)), dma((11,)), dma((11,)),
        ],
        compiler_params=pltpu.CompilerParams(
            collective_id=0, has_side_effects=True, vmem_limit_bytes=60 * 1024 * 1024
        ),
        cost_estimate=pl.CostEstimate(
            flops=4 * 8 * capacity * width * block, bytes_accessed=4 * width * block, transcendentals=0
        ),
    )(activations, active_blocks.T, enc_weight, enc_bias, dec_weight, dec_bias)
    return error, mean[0, 0]


def solution(mesh):
    in_specs = (P("lat", "tp"), P("lat", None), P("tp", "lat"), P("lat"), P("lat", "tp"), P("tp"))
    out_specs = (P("lat"), P())
    body = line_body if (mesh.shape["lat"], mesh.shape["tp"]) == (8, 4) else general_body
    return jax.shard_map(body, mesh=mesh, in_specs=in_specs, out_specs=out_specs, check_vma=False)
```

```python
import functools

import jax
import jax.numpy as jnp
from jax import lax
from jax.experimental import pallas as pl
from jax.experimental.pallas import tpu as pltpu
from jax.sharding import PartitionSpec as P


def score_slots(received, enc_weight, enc_bias, dec_weight):
    owners = received.shape[0]
    slot_count = received.shape[1]
    feature_part = received.shape[2]
    flat_rows = received.reshape(owners * slot_count, feature_part)
    partial_value = jnp.dot(flat_rows, enc_weight, preferred_element_type=jnp.float32)
    pre = lax.psum(partial_value.astype(jnp.bfloat16), "tp").astype(jnp.float32)
    latents = jnp.maximum(pre + enc_bias, 0.0).astype(jnp.bfloat16)
    decoded = jnp.dot(latents, dec_weight, preferred_element_type=jnp.float32).astype(jnp.bfloat16)
    decoded = decoded.reshape(owners, slot_count, feature_part)
    return lax.all_to_all(decoded, "lat", split_axis=0, concat_axis=0, tiled=True)


def finish(activations, summed, dec_bias, owners):
    token_count = activations.shape[0]
    recon = summed + dec_bias
    inputs_full = activations.astype(jnp.float32)
    diff = inputs_full - recon
    squares, norms = lax.psum(
        (jnp.sum(diff * diff, axis=1), jnp.sum(inputs_full * inputs_full, axis=1)), "tp"
    )
    token_error = squares / (norms + 1e-06)
    total = lax.psum(jnp.sum(token_error), "lat")
    mean_error = total / (token_count * owners)
    return (token_error, mean_error)


def general_body(activations, active_blocks, enc_weight, enc_bias, dec_weight, dec_bias):
    owners = lax.axis_size("lat")
    token_count, active_count = active_blocks.shape
    feature_part = activations.shape[1]
    capacity = 2 * token_count * active_count // owners
    centred = (activations.astype(jnp.float32) - dec_bias).astype(jnp.bfloat16)
    flat = active_blocks.reshape(-1)
    onehot = (flat[:, None] == jnp.arange(owners, dtype=jnp.int32)[None, :]).astype(jnp.int32)
    ranks = jnp.sum((jnp.cumsum(onehot, axis=0) - onehot) * onehot, axis=1)
    slot_rows = flat * capacity + ranks
    source_rows = jnp.repeat(centred, active_count, axis=0)
    outgoing = (
        jnp.zeros((owners * capacity, feature_part), jnp.bfloat16).at[slot_rows].set(source_rows)
    )
    outgoing = outgoing.reshape(owners, capacity, feature_part)
    received = lax.all_to_all(outgoing, "lat", split_axis=0, concat_axis=0, tiled=True)
    returned = score_slots(received, enc_weight, enc_bias, dec_weight)
    returned = returned.reshape(owners * capacity, feature_part)
    picked = returned[slot_rows].reshape(token_count, active_count, feature_part)
    return finish(activations, jnp.sum(picked.astype(jnp.float32), axis=1), dec_bias, owners)


MESH = pl.DeviceIdType.MESH
TILE = 256


def line_kernel(
    tokens, capacity,
    act, blocks, enc_hbm, enc_bias, dec_hbm, dec_bias,
    error_out, mean_out,
    enc, dec, src, meta, picks, places, rows, ysend, given, other, chip, side, lat,
    theirs, cat, part, from_mate, from_far, from_end, across2, across3,
    acc, norm, stats, stats_in, mean_own, mean_in,
    w_sem, hop_send, hop_recv, meta_send, meta_recv, col_send, col_recv, pair_send, pair_recv,
    back_send, back_recv, sum_send, sum_recv, end_send, end_recv,
):
    me, tp = lax.axis_index("lat"), lax.axis_index("tp")
    plane, column = me // 2, me % 2
    core = tp % 2
    inner = ((plane + 1) // 2) % 2 == 1
    outer = ((plane + 1) // 2) % 2 == 0
    width = act.shape[1]
    tiles = width // TILE
    half = enc.shape[1] // 2
    half_tiles = half // TILE

    def flip(value, mask):
        for bit in (1, 2, 4):
            if mask & bit:
                value = value + bit - 2 * bit * ((value // bit) % 2)
        return value

    def lat_peer(mask):
        return (flip(me, mask), tp)

    def tp_peer(mask):
        return (me, flip(tp, mask))

    MATE, ACROSS, OPPOSITE, COLUMN = 2, 6, 4, 1

    def columns(t, first=0):
        return pl.ds(pl.multiple_of(first + t * TILE, TILE), TILE)

    def remote(src_ref, dst_ref, send, recv, peer):
        return pltpu.make_async_remote_copy(
            src_ref=src_ref, dst_ref=dst_ref, send_sem=send, recv_sem=recv,
            device_id=peer, device_id_type=MESH,
        )

    enc_copy = pltpu.make_async_copy(enc_hbm, enc, w_sem.at[0])
    dec_copy = pltpu.make_async_copy(dec_hbm, dec, w_sem.at[1])
    enc_copy.start()
    dec_copy.start()

    def centre(t, carry):
        cols = pl.ds(pl.multiple_of(t * TILE, TILE), TILE)
        src[0, :, cols] = (act[:, cols].astype(jnp.float32) - dec_bias[cols][None]).astype(jnp.bfloat16)
        return carry

    lax.fori_loop(0, tiles, centre, 0)
    active_count = blocks.shape[0]
    meta[0, 0:active_count] = blocks[...]
    meta[0, active_count:8] = jnp.full((8 - active_count, tokens), -1, jnp.int32)

    barrier = pltpu.get_barrier_semaphore()
    for mask in range(1, 8):
        pl.semaphore_signal(barrier, inc=1, device_id=lat_peer(mask), device_id_type=MESH)
    for mask in range(1, 4):
        pl.semaphore_signal(barrier, inc=1, device_id=tp_peer(mask), device_id_type=MESH)
    pl.semaphore_wait(barrier, 10)

    far_slot = 3 - ((plane + 1) // 2) % 2
    meta_copies = [
        remote(meta.at[0], meta.at[1], meta_send.at[0], meta_recv.at[1], lat_peer(MATE)),
        remote(meta.at[0], meta.at[far_slot], meta_send.at[1], meta_recv.at[far_slot], lat_peer(ACROSS)),
        remote(meta.at[0], meta.at[far_slot], meta_send.at[2], meta_recv.at[far_slot], lat_peer(OPPOSITE)),
    ]
    for copy in meta_copies:
        copy.start()

    flows = [(0, 1, MATE), (0, 2, ACROSS), (2, 2, MATE), (1, 3, ACROSS), (3, 3, MATE)]

    def hop(flow, piece):
        here, there, mask = flows[flow]
        return remote(
            src.at[here, :, columns(piece)], src.at[there, :, columns(piece)],
            hop_send.at[flow, piece], hop_recv.at[there, piece], lat_peer(mask),
        )

    def each_tile(fn, first=0, last=tiles):
        lax.fori_loop(first, last, lambda t, carry: (fn(t), carry)[1], 0)

    def each_half_tile(fn):
        lax.fori_loop(0, half_tiles, lambda t, carry: (fn(t), carry)[1], 0)

    def first_hops(t):
        hop(0, t).start()

        @pl.when(inner)
        def _():
            hop(1, t).start()

    each_tile(first_hops)

    def squares_of_inputs(t):
        cols = pl.ds(pl.multiple_of(t * TILE, TILE), TILE)
        value = act[:, cols].astype(jnp.float32)
        norm[...] += value * value

    norm[...] = jnp.zeros_like(norm)
    acc[...] = jnp.zeros_like(acc)
    each_tile(squares_of_inputs)

    earlier = (
        lax.broadcasted_iota(jnp.int32, (tokens, tokens), 0)
        < lax.broadcasted_iota(jnp.int32, (tokens, tokens), 1)
    ).astype(jnp.float32).astype(jnp.bfloat16)
    slots = lax.broadcasted_iota(jnp.int32, (capacity, tokens), 0).astype(jnp.float32)

    def make_picks(k):
        names = meta[k]
        named = []
        for owner in (me, flip(me, COLUMN)):
            hit = jnp.max((names == owner).astype(jnp.float32), axis=0, keepdims=True)
            named.append(jnp.broadcast_to(hit, (8, tokens)))
        named = jnp.concatenate(named)
        ranks = jnp.dot(named.astype(jnp.bfloat16), earlier, preferred_element_type=jnp.float32)
        pick = jnp.concatenate([
            jnp.where(ranks[8 * i:8 * i + 1] == slots, named[8 * i:8 * i + 1], 0.0)
            for i in range(2)
        ])
        picks[k] = pick.astype(jnp.bfloat16)
        places[k] = pick.T.astype(jnp.bfloat16)

    def to_column(k, t):
        return remote(
            ysend.at[k, :, columns(t)], rows.at[k, pl.ds(capacity, capacity), columns(t)],
            col_send.at[k, t], col_recv.at[k, t], lat_peer(COLUMN),
        )

    def to_core(k, t):
        return remote(
            given.at[k, :, columns(t)], other.at[k, :, columns(t)],
            pair_send.at[0, k, t], pair_recv.at[0, k, t], tp_peer(1),
        )

    def to_side(k, t):
        return remote(
            chip.at[k, :, columns(t)], side.at[k, :, columns(t)],
            pair_send.at[1, k, t], pair_recv.at[1, k, t], tp_peer(2),
        )

    def to_core2(k, t):
        return remote(
            lat.at[k, core, :, columns(t)], lat.at[k, core, :, columns(t)],
            pair_send.at[2, k, t], pair_recv.at[2, k, t], tp_peer(1),
        )

    def pick_tile(k, t):
        got = jnp.dot(picks[k], src[k, :, columns(t)], preferred_element_type=jnp.float32)
        got = got.astype(jnp.bfloat16)
        rows[k, pl.ds(0, capacity), columns(t)] = got[:capacity]
        ysend[k, :, columns(t)] = got[capacity:]
        to_column(k, t).start()

    def encode(k):
        each_tile(lambda t: to_column(k, t).wait_recv())

        def give(t):
            cols = columns(t, (1 - core) * half)
            value = jnp.dot(rows[k], enc[:, cols], preferred_element_type=jnp.float32)
            given[k, :, columns(t)] = value.astype(jnp.bfloat16)
            to_core(k, t).start()

        def keep(t):
            cols = columns(t, core * half)
            value = jnp.dot(rows[k], enc[:, cols], preferred_element_type=jnp.float32)
            to_core(k, t).wait_recv()
            value += other[k, :, columns(t)].astype(jnp.float32)
            chip[k, :, columns(t)] = value.astype(jnp.bfloat16)
            to_side(k, t).start()

        each_half_tile(give)
        each_half_tile(keep)

    def activate(k):
        def tile(t):
            to_side(k, t).wait_recv()
            bias = enc_bias[columns(t, core * half)][None]
            pre = chip[k, :, columns(t)].astype(jnp.float32) + side[k, :, columns(t)].astype(jnp.float32)
            lat[k, core, :, columns(t)] = jnp.maximum(pre + bias, 0.0).astype(jnp.bfloat16)
            to_core2(k, t).start()

        each_half_tile(tile)

    def back(k, t):
        return remote(
            theirs.at[k, t], cat.at[k, t, pl.ds(capacity, capacity)],
            back_send.at[k, t], back_recv.at[k, t], lat_peer(COLUMN),
        )

    def wait_latents(k):
        each_half_tile(lambda t: to_core2(k, t).wait_recv())

    def decode_tile(k, t):
        cols = columns(t)
        value = jnp.dot(lat[k, 0], dec[pl.ds(0, half), cols], preferred_element_type=jnp.float32)
        value += jnp.dot(lat[k, 1], dec[pl.ds(half, half), cols], preferred_element_type=jnp.float32)
        value = value.astype(jnp.bfloat16)
        cat[k, t, pl.ds(0, capacity)] = value[:capacity]
        theirs[k, t] = value[capacity:]
        if k >= 1:
            back(k, t).start()

    sums = [(1, from_mate, MATE), (2, from_far, MATE), (3, from_end, MATE), (2, across2, ACROSS), (3, across3, ACROSS)]

    def pass_on(flow, t):
        k, target, mask = sums[flow]
        return remote(
            part.at[k, t], target.at[t], sum_send.at[flow, t], sum_recv.at[flow, t], lat_peer(mask)
        )

    def add_to_part(k, t, more):
        part[k, t] = (part[k, t].astype(jnp.float32) + more[t].astype(jnp.float32)).astype(jnp.bfloat16)

    def place_tile(k, t):
        back(k, t).wait_recv()
        value = jnp.dot(places[k], cat[k, t], preferred_element_type=jnp.float32)
        part[k, t] = value.astype(jnp.bfloat16)
        if k >= 1:
            @pl.when(outer)
            def _():
                pass_on(k - 1, t).start()

    LAG = 3

    def place_behind(k, t):
        @pl.when(t >= LAG)
        def _():
            place_tile(k, t - LAG)

    def place_rest(k):
        each_tile(lambda t: place_tile(k, t), tiles - LAG)

    meta_done = [
        remote(meta.at[0], meta.at[k], meta_send.at[0], meta_recv.at[k], lat_peer(MATE))
        for k in range(1, 4)
    ]

    make_picks(0)
    each_tile(lambda t: pick_tile(0, t))
    for k in range(1, 4):
        meta_done[k - 1].wait_recv()
        make_picks(k)

    def mate_arrives(t):
        @pl.when(inner)
        def _():
            hop(1, t).wait_recv()
            hop(2, t).start()

        hop(0, t).wait_recv()

        @pl.when(inner)
        def _():
            hop(3, t).start()

        pick_tile(1, t)

    def far_inner_arrives(t):
        @pl.when(outer)
        def _():
            hop(2, t).wait_recv()

        @pl.when(inner)
        def _():
            hop(3, t).wait_recv()
            hop(4, t).start()

        pick_tile(2, t)
        decode_tile(0, t)

    def far_outer_arrives(t):
        @pl.when(outer)
        def _():
            hop(3, t).wait_recv()

        pick_tile(3, t)

    def second_decode(t):
        decode_tile(1, t)
        place_behind(1, t)

    def third_decode(t):
        decode_tile(2, t)
        place_behind(2, t)

    def last_decode(t):
        decode_tile(3, t)

        @pl.when(outer)
        def _():
            place_behind(3, t)

    each_tile(mate_arrives, 0, tiles // 2)
    enc_copy.wait()
    encode(0)
    each_tile(mate_arrives, tiles // 2, tiles)
    encode(1)
    activate(0)
    dec_copy.wait()
    wait_latents(0)
    each_tile(far_inner_arrives, 0, tiles - 2)
    activate(1)
    each_tile(far_inner_arrives, tiles - 2, tiles)
    wait_latents(1)
    each_tile(second_decode)
    encode(2)
    place_rest(1)
    each_tile(far_outer_arrives)
    activate(2)
    encode(3)
    wait_latents(2)
    each_tile(third_decode)
    place_rest(2)
    activate(3)
    wait_latents(3)
    each_tile(last_decode)
    each_tile(lambda t: back(0, t).start())

    @pl.when(outer)
    def _():
        place_rest(3)
        each_tile(lambda t: place_tile(0, t))

    @pl.when(inner)
    def _():
        def far_tile(t):
            pass_on(1, t).wait_recv()
            add_to_part(2, t, from_far)
            pass_on(3, t).start()
            place_tile(0, t)

        def last_hop(t):
            pass_on(4, t).wait_recv()
            add_to_part(1, t, across3)
            pass_on(0, t).start()

        def end_tile(t):
            place_tile(3, t)
            pass_on(2, t).wait_recv()
            add_to_part(3, t, from_end)
            pass_on(4, t).start()

            @pl.when(t >= 1)
            def _():
                last_hop(t - 1)

        each_tile(far_tile)
        each_tile(end_tile)
        last_hop(tiles - 1)

    def finish_tile(t):
        pass_on(0, t).wait_recv()
        cols = pl.ds(pl.multiple_of(t * TILE, TILE), TILE)
        diff = act[:, cols].astype(jnp.float32) - dec_bias[cols][None]
        diff = diff - part[0, t].astype(jnp.float32) - from_mate[t].astype(jnp.float32)
        return diff

    @pl.when(outer)
    def _():
        def tile(t):
            diff = finish_tile(t)
            acc[...] += diff * diff

        each_tile(tile)

    @pl.when(inner)
    def _():
        def tile(t):
            pass_on(3, t).wait_recv()
            diff = finish_tile(t) - across2[t].astype(jnp.float32)
            acc[...] += diff * diff

        each_tile(tile)

    stats[0:1] = jnp.sum(acc[...].T, axis=0, keepdims=True)
    stats[1:2] = jnp.sum(norm[...].T, axis=0, keepdims=True)
    stats[2:8] = jnp.zeros((6, tokens), jnp.float32)
    stat_copies = [
        remote(stats, stats_in.at[m], end_send.at[m], end_recv.at[m], tp_peer(m)) for m in range(1, 4)
    ]
    for copy in stat_copies:
        copy.start()
    for copy in stat_copies:
        copy.wait()
    both = (stats[...] + stats_in[1]) + (stats_in[2] + stats_in[3])
    error = both[0:1] / (both[1:2] + 1e-06)
    error_out[...] = error[0]
    mean_own[...] = jnp.broadcast_to(jnp.sum(error, axis=1, keepdims=True), (8, 128))
    mean_copies = [
        remote(mean_own, mean_in.at[m], end_send.at[3 + m], end_recv.at[3 + m], lat_peer(m))
        for m in range(1, 8)
    ]
    for copy in mean_copies:
        copy.start()
    for copy in mean_copies:
        copy.wait()
    low = (mean_own[...] + mean_in[1]) + (mean_in[2] + mean_in[3])
    high = (mean_in[4] + mean_in[5]) + (mean_in[6] + mean_in[7])
    mean_out[0, 0] = jnp.max((low + high) / (tokens * 8))

    for copy in meta_copies:
        copy.wait_send()
    each_tile(lambda t: hop(0, t).wait_send())
    for k in range(4):
        each_tile(lambda t: to_column(k, t).wait_send())
        for flow in (to_core, to_side, to_core2):
            each_half_tile(lambda t: flow(k, t).wait_send())
        each_tile(lambda t: back(k, t).wait_send())
    each_tile(lambda t: pass_on(0, t).wait_send())

    @pl.when(inner)
    def _():
        for flow in range(1, 5):
            each_tile(lambda t: hop(flow, t).wait_send())
        for flow in (3, 4):
            each_tile(lambda t: pass_on(flow, t).wait_send())

    @pl.when(outer)
    def _():
        for flow in (1, 2):
            each_tile(lambda t: pass_on(flow, t).wait_send())


def line_body(activations, active_blocks, enc_weight, enc_bias, dec_weight, dec_bias):
    tokens, active_count = active_blocks.shape
    capacity = 2 * tokens * active_count // 8
    width = activations.shape[1]
    block = enc_weight.shape[1]
    half = block // 2
    tiles = width // TILE
    bf, f32 = jnp.bfloat16, jnp.float32
    vm, dma = pltpu.VMEM, pltpu.SemaphoreType.DMA
    in_vmem = pl.BlockSpec(memory_space=pltpu.VMEM)
    anywhere = pl.BlockSpec(memory_space=pl.ANY)
    tiled = (tiles, tokens, TILE)
    error, mean = pl.pallas_call(
        functools.partial(line_kernel, tokens, capacity),
        out_shape=(jax.ShapeDtypeStruct((tokens,), f32), jax.ShapeDtypeStruct((1, 1), f32)),
        in_specs=[in_vmem, in_vmem, anywhere, in_vmem, anywhere, in_vmem],
        out_specs=(in_vmem, pl.BlockSpec(memory_space=pltpu.SMEM)),
        scratch_shapes=[
            vm((width, block), bf), vm((block, width), bf),
            vm((4, tokens, width), bf), vm((4, 8, tokens), jnp.int32),
            vm((4, 2 * capacity, tokens), bf), vm((4, tokens, 2 * capacity), bf),
            vm((4, 2 * capacity, width), bf), vm((4, capacity, width), bf),
            vm((4, 2 * capacity, half), bf), vm((4, 2 * capacity, half), bf),
            vm((4, 2 * capacity, half), bf), vm((4, 2 * capacity, half), bf),
            vm((4, 2, 2 * capacity, half), bf),
            vm((4, tiles, capacity, TILE), bf), vm((4, tiles, 2 * capacity, TILE), bf),
            vm((4,) + tiled, bf),
            vm(tiled, bf), vm(tiled, bf), vm(tiled, bf), vm(tiled, bf), vm(tiled, bf),
            vm((tokens, TILE), f32), vm((tokens, TILE), f32),
            vm((8, tokens), f32), vm((4, 8, tokens), f32), vm((8, 128), f32), vm((8, 8, 128), f32),
            dma((2,)), dma((5, tiles)), dma((4, tiles)), dma((3,)), dma((4,)),
            dma((4, tiles)), dma((4, tiles)), dma((3, 4, half // TILE)), dma((3, 4, half // TILE)),
            dma((4, tiles)), dma((4, tiles)),
            dma((5, tiles)), dma((5, tiles)), dma((11,)), dma((11,)),
        ],
        compiler_params=pltpu.CompilerParams(
            collective_id=0, has_side_effects=True, vmem_limit_bytes=60 * 1024 * 1024
        ),
        cost_estimate=pl.CostEstimate(
            flops=4 * 8 * capacity * width * block, bytes_accessed=4 * width * block, transcendentals=0
        ),
    )(activations, active_blocks.T, enc_weight, enc_bias, dec_weight, dec_bias)
    return error, mean[0, 0]


def solution(mesh):
    in_specs = (P("lat", "tp"), P("lat", None), P("tp", "lat"), P("lat"), P("lat", "tp"), P("tp"))
    out_specs = (P("lat"), P())
    body = line_body if (mesh.shape["lat"], mesh.shape["tp"]) == (8, 4) else general_body
    return jax.shard_map(body, mesh=mesh, in_specs=in_specs, out_specs=out_specs, check_vma=False)
```
